32 devices in a mesh: gx: 4 (over z), gy: 8 (over y, x, core).
Axes of the slice: x: 2, y: 2, z: 4, core: 2. Of those that a mesh axis runs over, the one named last changes fastest.
Arguments:
- media_features: bfloat16 [64, 256, 1536], P(('gx', 'gy')), may hold values from -6 to 6
- latents: bfloat16 [64, 64, 1536], P(('gx', 'gy')), may hold values from -6 to 6
- cotangent: bfloat16 [64, 64, 1536], P(('gx', 'gy')), may hold values from -6 to 6
- image_counts: int32 [32], P(('gx', 'gy')), may hold values from 1 to 2, 48 in all
- w_query: bfloat16 [1536, 1536], P(('gx', 'gy')), may hold values from -0.15625 to 0.15625
- w_key: bfloat16 [1536, 1536], P(('gx', 'gy')), may hold values from -0.15625 to 0.15625
- w_value: bfloat16 [1536, 1536], P(('gx', 'gy')), may hold values from -0.15625 to 0.15625
- w_out: bfloat16 [1536, 1536], P(None, ('gx', 'gy')), may hold values from -0.625 to 0.625
- w_up: bfloat16 [1536, 6144], P(('gx', 'gy')), may hold values from -0.15625 to 0.15625
- w_down: bfloat16 [6144, 1536], P(None, ('gx', 'gy')), may hold values from -0.078125 to 0.078125
- norm_gains: float32 [3, 1536], P(None, ('gx', 'gy')), may hold values from 0.1 to 1.9
- norm_biases: float32 [3, 1536], P(None, ('gx', 'gy')), may hold values from -2 to 2
Outputs:
- latents_out: bfloat16 [64, 64, 1536], P(('gx', 'gy'))
- grad_media: float32 [64, 256, 1536], P(('gx', 'gy'))
- grad_latents: float32 [64, 64, 1536], P(('gx', 'gy'))
- grad_w_query: float32 [1536, 1536], P(('gx', 'gy'))
- grad_w_key: float32 [1536, 1536], P(('gx', 'gy'))
- grad_w_value: float32 [1536, 1536], P(('gx', 'gy'))
- grad_w_out: float32 [1536, 1536], P(None, ('gx', 'gy'))
- grad_w_up: float32 [1536, 6144], P(('gx', 'gy'))
- grad_w_down: float32 [6144, 1536], P(None, ('gx', 'gy'))
- grad_norm_gains: float32 [3, 1536], P(None, ('gx', 'gy'))
- grad_norm_biases: float32 [3, 1536], P(None, ('gx', 'gy'))
The draws below stay inside these ranges and needn't reach their ends.
Inputs may be any that keep to these rules, and one draw needn't show every extreme that they name: image_counts[d] is the number of images of the sequence held by device d (index d of gx+gy); they fill the first image_counts[d] slots of that device, the other slots hold unused data. The counts sum to 48 and some device is full.
All inputs are finite; a program needn't handle non-finite values.
Results may differ from the reference program's by a relative error of at most 0.033.
Values may be sent and summed in bfloat16 or wider, within the bound.
No kernel may reach another device: no remote copies, remote signals or barrier semaphores. Data moves between devices by JAX's collectives and lax.ppermute only.
A program may use at most 320 MiB of HBM per device.

```python
import math
import jax
import jax.numpy as jnp
import numpy as np
from jax import lax

D = 1536
HEADS = 16
HEAD = 96
FF = 6144
LAT = 64
PATCH = 256
IMG_DEV = 2
SLOTS = 64
LIVE = 48
N_GX = 4
N_GY = 8


def level_of(key, extent, split, low, top_value):
    gain, own = 1.0, jax.random.fold_in(key, 6)
    for position, shards_of in split:
        heights = jnp.exp(jax.random.uniform(jax.random.fold_in(own, position), (shards_of,), jnp.float32, low / len(split), top_value / len(split)))
        gain = gain * jnp.repeat(heights, extent[position] // shards_of).reshape([-1 if axis == position else 1 for axis in range(len(extent))])
    return gain


def length_profile(count, total, bound, lean):
    loads = [(1 << 20) // math.isqrt(rank ** lean) + 1 for rank in range(2, count + 1)]
    spare, counts = total - bound - (count - 1), [1] * (count - 1)
    while spare > 0:
        movable = [i for i in range(count - 1) if counts[i] < bound]
        pool, remaining = sum([loads[i] for i in movable]), spare
        for i in movable:
            more = min(bound - counts[i], max(1, remaining * loads[i] // pool), spare)
            counts[i] = counts[i] + more
            spare = spare - more
    return np.array([bound] + counts)


def ragged_sizes(stream_key, amount, total, bound, skew):
    if amount == 2:
        one = jax.random.randint(stream_key, (), max(1, total - bound), min(bound, total - 1) + 1)
        return jnp.stack([one, total - one])
    sizes = jnp.asarray(length_profile(amount, total, bound, skew), jnp.int32)
    twos = (amount - 1) // 2
    giver, receiver = sizes[1:1 + 2 * twos:2], sizes[2:2 + 2 * twos:2]
    room = jnp.minimum(giver - 1, bound - receiver)
    moved = jax.random.randint(jax.random.fold_in(stream_key, 1), (twos,), 0, 1 << 20) % (room + 1)
    sizes = sizes.at[1:1 + 2 * twos:2].set(giver - moved).at[2:2 + 2 * twos:2].set(receiver + moved)
    return sizes[jax.random.permutation(jax.random.fold_in(stream_key, 2), amount)]


def scatter_about(stream_key, shape, scale, bound, shards=(), kind=jnp.bfloat16):
    gain = level_of(stream_key, shape, shards, -0.22, 0.18) if shards else 1.0
    entries = jax.random.normal(stream_key, shape, jnp.float32) * scale * gain
    return jnp.minimum(jnp.maximum(entries, -bound), bound).astype(kind)


def setup_inputs(seed: int = 0) -> dict:
    seeds = jax.random.split(jax.random.key(seed), 13)
    return {
        "media_features": scatter_about(seeds[0], (SLOTS, PATCH, D), 1.0, 6.0, ((0, 32),)),
        "latents": scatter_about(seeds[1], (SLOTS, LAT, D), 1.0, 6.0, ((0, 32),)),
        "cotangent": scatter_about(seeds[2], (SLOTS, LAT, D), 1.0, 6.0, ((0, 32),)),
        "image_counts": ragged_sizes(seeds[3], N_GX * N_GY, LIVE, IMG_DEV, 2).astype(jnp.int32),
        "w_query": scatter_about(seeds[4], (D, D), D ** -0.5, 0.15625, ((0, 32),)),
        "w_key": scatter_about(seeds[5], (D, D), D ** -0.5, 0.15625, ((0, 32),)),
        "w_value": scatter_about(seeds[6], (D, D), D ** -0.5, 0.15625, ((0, 32),)),
        "w_out": scatter_about(seeds[7], (D, D), (D // 16) ** -0.5, 0.625, ((1, 32),)),
        "w_up": scatter_about(seeds[8], (D, FF), D ** -0.5, 0.15625, ((0, 32),)),
        "w_down": scatter_about(seeds[9], (FF, D), FF ** -0.5, 0.078125, ((1, 32),)),
        "norm_gains": jnp.clip(1.0 + 0.18 * jax.random.normal(seeds[10], (3, D), jnp.float32), 0.1, 1.9),
        "norm_biases": scatter_about(seeds[11], (3, D), 0.3, 2.0, ((1, 32),), jnp.float32),
    }


@jax.custom_vjp
def low(v):
    return lax.optimization_barrier(v.astype(jnp.bfloat16)).astype(jnp.float32)

@jax.custom_vjp
def low_back(v):
    return v

def low_keep(v):
    return (low(v), None)

def low_pass(kept, grad):
    return (grad,)

def back_keep(v):
    return (v, None)

def back_low(kept, grad):
    return (low(grad),)
low.defvjp(low_keep, low_pass)
low_back.defvjp(back_keep, back_low)
EPSILON = 1e-05

def exact_product(left, right):
    return jnp.dot(left, right, precision=lax.Precision.HIGHEST, preferred_element_type=jnp.float32)

def layer_norm(rows, gain_row, bias_row):
    average = lax.optimization_barrier(jnp.mean(rows, axis=-1, keepdims=True))
    centred = rows - average
    spread = lax.optimization_barrier(jnp.mean(centred * centred, axis=-1, keepdims=True))
    return centred * lax.rsqrt(spread + EPSILON) * gain_row + bias_row

def one_image(parameters, media_rows, latent_rows):
    w_query, w_key, w_value, w_out, w_up, w_down, gains, biases = parameters
    media_norm = low(layer_norm(media_rows, gains[0], biases[0]))
    latent_norm = low(layer_norm(latent_rows, gains[1], biases[1]))
    joined = jnp.concatenate([media_norm, latent_norm], axis=0)
    query = low_back(low(exact_product(latent_norm, w_query) * HEAD ** (-0.5)))
    keys = low_back(low(exact_product(joined, w_key)))
    values = low_back(low(exact_product(joined, w_value)))
    query_heads = query.reshape(LAT, HEADS, HEAD)
    key_heads = keys.reshape(PATCH + LAT, HEADS, HEAD)
    value_heads = values.reshape(PATCH + LAT, HEADS, HEAD)
    scores = low_back(jnp.einsum('qhd,khd->hqk', query_heads, key_heads, precision=lax.Precision.HIGHEST))
    probs = low(jax.nn.softmax(scores, axis=-1))
    mixed = jnp.einsum('hqk,khd->qhd', probs, value_heads, precision=lax.Precision.HIGHEST)
    mixed = low_back(low(mixed.reshape(LAT, D)))
    attended = latent_rows + low_back(exact_product(mixed, w_out))
    hidden = low(layer_norm(attended, gains[2], biases[2]))
    upper = low_back(exact_product(hidden, w_up))
    active = low(jax.nn.gelu(upper, approximate=False))
    return attended + low_back(exact_product(active, w_down))

def reference(media_features, latents, cotangent, image_counts, w_query, w_key, w_value, w_out, w_up, w_down, norm_gains, norm_biases):
    devices_total = image_counts.shape[0]
    slot_index = jnp.arange(SLOTS, dtype=jnp.int32)
    live_mask = (slot_index % IMG_DEV < image_counts[slot_index // IMG_DEV]).astype(jnp.float32)
    live_blocks = live_mask.reshape(devices_total, IMG_DEV)
    parameters = (w_query.astype(jnp.float32), w_key.astype(jnp.float32), w_value.astype(jnp.float32), w_out.astype(jnp.float32), w_up.astype(jnp.float32), w_down.astype(jnp.float32), norm_gains, norm_biases)
    media_blocks = media_features.astype(jnp.float32).reshape(devices_total, IMG_DEV, PATCH, D)
    latent_blocks = latents.astype(jnp.float32).reshape(devices_total, IMG_DEV, LAT, D)

    def forward(weights, media_all, latent_all):

        def device_block(pieces):
            media_piece, latent_piece, keep_mask = pieces
            result = jax.vmap(one_image, in_axes=(None, 0, 0))(weights, media_piece, latent_piece)
            return result * keep_mask[:, None, None]
        return lax.map(jax.checkpoint(device_block), (media_all, latent_all, live_blocks))
    result, pullback = jax.vjp(forward, parameters, media_blocks, latent_blocks)
    cot_blocks = cotangent.astype(jnp.float32).reshape(devices_total, IMG_DEV, LAT, D)
    grad_parameters, grad_media, grad_latents = pullback(cot_blocks)
    return (result.reshape(SLOTS, LAT, D).astype(jnp.bfloat16), grad_media.reshape(SLOTS, PATCH, D), grad_latents.reshape(SLOTS, LAT, D), grad_parameters[0], grad_parameters[1], grad_parameters[2], grad_parameters[3], grad_parameters[4], grad_parameters[5], grad_parameters[6], grad_parameters[7])
```

```python
import functools

import jax
import jax.numpy as jnp
from jax import lax
from jax.experimental import pallas as pl
from jax.experimental.pallas import tpu as pltpu
from jax.sharding import PartitionSpec as P

HEAD = 96
LANES = 128
EPSILON = 1e-05
BF16 = jnp.bfloat16
F32 = jnp.float32


def product(left, right):
    return jnp.dot(left, right, preferred_element_type=F32)


def product_left(left, right):
    return lax.dot_general(left, right, (((0,), (0,)), ((), ())), preferred_element_type=F32)


def product_right(left, right):
    return lax.dot_general(left, right, (((1,), (1,)), ((), ())), preferred_element_type=F32)


def swap(block, mask, axis="gy"):
    count = lax.axis_size(axis)
    return lax.ppermute(block, axis, [(i, i ^ mask) for i in range(count)])


def far_masks():
    return [mask for mask in range(lax.axis_size("gy")) if mask % 2 == 0]


def spread(block):
    far = jnp.stack([block] + [swap(block, mask) for mask in far_masks()[1:]])
    return jnp.concatenate([far, swap(far, 1)])


def collect(parts):
    count = parts.shape[0] // 2
    own = (parts[:count].astype(F32) + swap(parts[count:], 1).astype(F32)).astype(BF16)
    total = own[0].astype(F32)
    for index, mask in enumerate(far_masks()[1:]):
        total = total + swap(own[1 + index], mask).astype(F32)
    return total


def far_bits():
    bits, bit = [], 2
    while bit < lax.axis_size("gy"):
        bits.append(bit)
        bit *= 2
    return bits


def route(turn):
    bits = far_bits()
    turn = turn % len(bits)
    return bits[turn:] + bits[:turn]


def spread_big(block, turn):
    held = {0: block}
    for bit in route(turn):
        held.update({mask ^ bit: swap(part, bit) for mask, part in list(held.items())})
    return held


def collect_big(parts, turn):
    held = dict(parts)
    for bit in reversed(route(turn)):
        for mask in [m for m in held if not m & bit]:
            arrived = swap(held.pop(mask ^ bit), bit)
            held[mask] = (held[mask].astype(F32) + arrived.astype(F32)).astype(BF16)
    return held[0]


def bits_of(count):
    bits, bit = [], 1
    while bit < count:
        bits.append(bit)
        bit *= 2
    return bits


def gather_small(rows):
    for axis in ("gy", "gx"):
        place = lax.axis_index(axis)
        for bit in bits_of(lax.axis_size(axis)):
            other = swap(rows, bit, axis)
            upper = (place & bit) != 0
            rows = jnp.concatenate([jnp.where(upper, other, rows), jnp.where(upper, rows, other)])
    return rows


def sum_small(rows):
    for axis in ("gy", "gx"):
        for bit in bits_of(lax.axis_size(axis)):
            rows = rows + swap(rows, bit, axis)
    return rows


def normed(rows, gain, bias):
    average = jnp.mean(rows, axis=-1, keepdims=True)
    centred = rows - average
    spread_of = jnp.mean(centred * centred, axis=-1, keepdims=True)
    return centred * lax.rsqrt(spread_of + EPSILON) * gain + bias


def head_mask(rows, lanes, head):
    lane = lax.broadcasted_iota(jnp.int32, (rows, lanes), 1)
    return (lane >= head * HEAD) & (lane < (head + 1) * HEAD)


def stacked(rows, heads):
    count, lanes = rows.shape
    return jnp.concatenate(
        [jnp.where(head_mask(count, lanes, h), rows, jnp.zeros_like(rows)) for h in range(heads)]
    )


def unstacked(rows, heads):
    count, lanes = rows.shape[0] // heads, rows.shape[1]
    total = jnp.zeros((count, lanes), rows.dtype)
    for h in range(heads):
        total = jnp.where(head_mask(count, lanes, h), rows[h * count : (h + 1) * count], total)
    return total


def softmax_rows(scores):
    top = jnp.max(scores, axis=-1, keepdims=True)
    raised = jnp.exp(scores - top)
    return raised / jnp.sum(raised, axis=-1, keepdims=True)


def attend_kernel(heads, patch, scale, media_ref, latent_ref, gains_ref, biases_ref, weights_ref,
                  joined_ref, kv_ref, query_ref, mixed_ref, out_ref):
    lanes = weights_ref.shape[1] // 4
    media = normed(media_ref[0].astype(F32), gains_ref[0:1], biases_ref[0:1]).astype(BF16)
    latent = normed(latent_ref[0].astype(F32), gains_ref[1:2], biases_ref[1:2]).astype(BF16)
    joined_ref[0, :patch] = media
    joined_ref[0, patch:] = latent
    kv_ref[0, :patch] = product(media, weights_ref[:, : 2 * lanes]).astype(BF16)
    kv_ref[0, patch:] = product(latent, weights_ref[:, : 2 * lanes]).astype(BF16)
    query = (product(latent, weights_ref[:, 2 * lanes : 3 * lanes]) * scale).astype(BF16)
    query_ref[0] = query
    keys, values = kv_ref[0, :, :lanes], kv_ref[0, :, lanes:]
    probs = softmax_rows(product_right(stacked(query, heads), keys))
    mixed = unstacked(product(probs.astype(BF16), values), heads).astype(BF16)
    mixed_ref[0] = mixed
    out_ref[0] = product_right(mixed, weights_ref[:, 3 * lanes :]).astype(BF16)


def attend(media, latent, gains, biases, weights, heads):
    count, patch, width = media.shape
    lat = latent.shape[1]
    lanes = weights.shape[1] // 4
    rows = patch + lat
    whole = lambda shape: pl.BlockSpec(shape, lambda i: (0,) * len(shape))
    one = lambda *shape: pl.BlockSpec((1,) + shape, lambda i: (i, 0, 0))
    return pl.pallas_call(
        functools.partial(attend_kernel, heads, patch, HEAD ** (-0.5)),
        grid=(count,),
        in_specs=[one(patch, width), one(lat, width), whole(gains.shape), whole(biases.shape), whole(weights.shape)],
        out_specs=[one(rows, width), one(rows, 2 * lanes), one(lat, lanes), one(lat, lanes), one(lat, width)],
        out_shape=[
            jax.ShapeDtypeStruct((count, rows, width), BF16),
            jax.ShapeDtypeStruct((count, rows, 2 * lanes), BF16),
            jax.ShapeDtypeStruct((count, lat, lanes), BF16),
            jax.ShapeDtypeStruct((count, lat, lanes), BF16),
            jax.ShapeDtypeStruct((count, lat, width), BF16),
        ],
        compiler_params=pltpu.CompilerParams(vmem_limit_bytes=48 * 2**20),
        cost_estimate=pl.CostEstimate(
            flops=2 * count * rows * width * 3 * lanes, bytes_accessed=4 * count * rows * width, transcendentals=0
        ),
    )(media, latent, gains, biases, weights)


def attend_back_kernel(heads, patch, scale, branch_ref, kv_ref, query_ref, weights_ref, joined_ref, dkv_ref, dquery_ref):
    lanes = weights_ref.shape[1] // 4
    query = stacked(query_ref[0], heads)
    keys, values = kv_ref[0, :, :lanes], kv_ref[0, :, lanes:]
    probs = softmax_rows(product_right(query, keys))
    grad_mixed = product(branch_ref[0], weights_ref[:, 3 * lanes :]).astype(BF16)
    grad_mixed = stacked(grad_mixed, heads)
    grad_values = product_left(probs.astype(BF16), grad_mixed).astype(BF16)
    grad_probs = product_right(grad_mixed, values)
    inner = jnp.sum(grad_probs * probs, axis=-1, keepdims=True)
    grad_scores = (probs * (grad_probs - inner)).astype(BF16)
    grad_query = unstacked(product(grad_scores, keys), heads).astype(BF16)
    grad_keys = product_left(grad_scores, query).astype(BF16)
    dkv_ref[0, :, :lanes] = grad_keys
    dkv_ref[0, :, lanes:] = grad_values
    dquery_ref[0] = grad_query
    back = product_right(grad_keys, weights_ref[:, :lanes]) + product_right(grad_values, weights_ref[:, lanes : 2 * lanes])
    extra = product_right(grad_query, weights_ref[:, 2 * lanes : 3 * lanes]) * scale
    joined_ref[0, :patch] = back[:patch].astype(BF16)
    joined_ref[0, patch:] = (back[patch:] + extra).astype(BF16)


def attend_back(branch, kv, query, weights, heads):
    count, lat, width = branch.shape
    rows, lanes = kv.shape[1], weights.shape[1] // 4
    whole = lambda shape: pl.BlockSpec(shape, lambda i: (0,) * len(shape))
    one = lambda *shape: pl.BlockSpec((1,) + shape, lambda i: (i, 0, 0))
    return pl.pallas_call(
        functools.partial(attend_back_kernel, heads, rows - lat, HEAD ** (-0.5)),
        grid=(count,),
        in_specs=[one(lat, width), one(rows, 2 * lanes), one(lat, lanes), whole(weights.shape)],
        out_specs=[one(rows, width), one(rows, 2 * lanes), one(lat, lanes)],
        out_shape=[
            jax.ShapeDtypeStruct((count, rows, width), BF16),
            jax.ShapeDtypeStruct((count, rows, 2 * lanes), BF16),
            jax.ShapeDtypeStruct((count, lat, lanes), BF16),
        ],
        compiler_params=pltpu.CompilerParams(vmem_limit_bytes=48 * 2**20),
        cost_estimate=pl.CostEstimate(
            flops=2 * count * rows * width * 3 * lanes, bytes_accessed=3 * count * rows * width, transcendentals=0
        ),
    )(branch, kv, query, weights)


def norm_back(rows, gain, grad):
    average = jnp.mean(rows, axis=-1, keepdims=True)
    centred = rows - average
    inverse = lax.rsqrt(jnp.mean(centred * centred, axis=-1, keepdims=True) + EPSILON)
    unit = centred * inverse
    scaled = grad * gain
    first = jnp.mean(scaled, axis=-1, keepdims=True)
    second = jnp.mean(scaled * unit, axis=-1, keepdims=True)
    back = inverse * (scaled - first - unit * second)
    axes = tuple(range(rows.ndim - 1))
    return back, jnp.sum(grad * unit, axis=axes), jnp.sum(grad, axis=axes)


def local(media_features, latents, cotangent, image_counts, w_query, w_key, w_value, w_out, w_up, w_down,
          norm_gains, norm_biases):
    devices_x, devices_y = lax.axis_size("gx"), lax.axis_size("gy")
    img_count, lat, width = latents.shape
    patch = media_features.shape[1]
    rows = patch + lat
    shard = w_query.shape[0]
    head_width = width // devices_y
    heads = head_width // HEAD
    ff_width = w_up.shape[1] // devices_y
    lanes = -(-head_width // LANES) * LANES

    four = jnp.stack([w_key, w_value, w_query, w_out.T])
    four = four.reshape(4, shard, devices_y, head_width).transpose(2, 1, 0, 3).reshape(devices_y, shard, 4 * head_width)
    four = lax.all_to_all(four, "gy", split_axis=0, concat_axis=0, tiled=True)
    four = lax.all_gather(four.reshape(devices_y * shard, 4 * head_width), "gx", axis=0, tiled=True)
    weights = jnp.pad(four.reshape(width, 4, head_width), ((0, 0), (0, 0), (0, lanes - head_width)))
    weights = weights.reshape(width, 4 * lanes)

    two = jnp.stack([w_up, w_down.T]).reshape(2, shard, devices_y, ff_width).transpose(2, 0, 1, 3)
    two = lax.all_to_all(two, "gy", split_axis=0, concat_axis=0, tiled=True)
    up_cols = lax.all_gather(two[:, 0].reshape(devices_y * shard, ff_width), "gx", axis=0, tiled=True)
    down_cols = lax.all_gather(two[:, 1].reshape(devices_y * shard, ff_width), "gx", axis=0, tiled=True)

    small = jnp.stack([norm_gains, norm_biases]).reshape(1, 6 * shard)
    small = gather_small(small).reshape(devices_x * devices_y, 2, 3, shard).transpose(1, 2, 0, 3).reshape(2, 3, width)
    gains, biases = small[0], small[1]

    own = jnp.concatenate([media_features, latents], axis=1)
    pieces = []
    for image in range(img_count):
        held = spread_big(own[image], image)
        for mask in far_masks():
            pieces.append((image, mask, jnp.stack([held[mask], swap(held[mask], 1)])))

    live = (jnp.arange(img_count, dtype=jnp.int32) < image_counts[0]).astype(BF16)
    cot_own = cotangent * live[:, None, None]
    cot_all = spread(cot_own)

    done = {}
    for image, mask, piece in pieces:
        done[image, mask] = attend(piece[:, :patch], piece[:, patch:], gains, biases, weights, heads)

    def in_order(position):
        near = [jnp.stack([done[image, mask][position][0] for image in range(img_count)]) for mask in far_masks()]
        far = [jnp.stack([done[image, mask][position][1] for image in range(img_count)]) for mask in far_masks()]
        return jnp.stack(near + far)

    latent_float = latents.astype(F32)
    attended = collect(in_order(4)) + latent_float
    hidden_own = normed(attended, gains[2], biases[2]).astype(BF16)
    hidden = spread(hidden_own).reshape(-1, width)
    group = devices_y * img_count

    upper = product(hidden, up_cols)
    cdf = 0.5 * (1.0 + lax.erf(upper * (0.5**0.5)))
    active = (upper * cdf).astype(BF16)
    slope = cdf + upper * jnp.exp(-0.5 * upper * upper) * (0.5 / jnp.pi) ** 0.5
    cot_flat = cot_all.reshape(-1, width)
    grad_upper = (slope * product(cot_flat, down_cols)).astype(BF16)
    hidden_parts = product_right(grad_upper, up_cols).astype(BF16)
    grad_hidden = collect(hidden_parts.reshape(devices_y, img_count, lat, width))
    ffn_parts = product_right(active, down_cols).astype(BF16)
    result = attended + collect(ffn_parts.reshape(devices_y, img_count, lat, width))
    outputs = (result * live.astype(F32)[:, None, None]).astype(BF16)

    def home(grads, count):
        part = lax.psum_scatter(grads.astype(BF16), "gx", scatter_dimension=0, tiled=True)
        part = part.reshape(devices_y, shard, -1)
        part = lax.all_to_all(part, "gy", split_axis=0, concat_axis=0, tiled=True)
        part = part.reshape(devices_y, shard, count, -1).transpose(2, 1, 0, 3).reshape(count, shard, -1)
        return part.astype(F32)

    grad_down = home(product_left(cot_flat, active), 1)[0]
    grad_up = home(product_left(hidden, grad_upper), 1)[0]

    grad_norm_input, gain_two, bias_two = norm_back(attended, gains[2], grad_hidden)
    grad_attended = cot_own.astype(F32) + grad_norm_input
    branch = spread(grad_attended.astype(BF16))

    grads = {}
    count = len(far_masks())
    for image, mask, piece in pieces:
        index = far_masks().index(mask)
        pair = jnp.stack([branch[index, image], branch[count + index, image]])
        grads[image, mask] = attend_back(pair, done[image, mask][1], done[image, mask][2], weights, heads)

    back = []
    for image in range(img_count):
        parts = {}
        for mask in far_masks():
            both = grads[image, mask][0]
            parts[mask] = (both[0].astype(F32) + swap(both[1], 1).astype(F32)).astype(BF16)
        back.append(collect_big(parts, image))
    grad_joined = jnp.stack(back).astype(F32)

    keys = [(image, mask) for image, mask, _ in pieces]
    joined_all = jnp.concatenate([done[key][0] for key in keys]).reshape(-1, width)
    latent_all = jnp.concatenate([done[key][0][:, patch:] for key in keys]).reshape(-1, width)
    mixed_all = jnp.concatenate([done[key][3] for key in keys]).reshape(-1, lanes)
    dkv_all = jnp.concatenate([grads[key][1] for key in keys]).reshape(-1, 2 * lanes)
    dquery_all = jnp.concatenate([grads[key][2] for key in keys]).reshape(-1, lanes)
    branch_all = jnp.concatenate(
        [jnp.stack([branch[far_masks().index(mask), image], branch[count + far_masks().index(mask), image]]) for image, mask in keys]
    ).reshape(-1, width)
    dkv_cols = product_left(joined_all, dkv_all).reshape(width, 2, lanes)[:, :, :head_width].reshape(width, -1)
    dquery_cols = product_left(latent_all, dquery_all)[:, :head_width] * HEAD ** (-0.5)
    dout_cols = product_left(branch_all, mixed_all)[:, :head_width]
    grad_key, grad_value, grad_query, grad_out = home(
        jnp.concatenate([dkv_cols, dquery_cols, dout_cols], axis=1), 4
    )

    grad_media, gain_zero, bias_zero = norm_back(media_features.astype(F32), gains[0], grad_joined[:, :patch])
    grad_latent, gain_one, bias_one = norm_back(latent_float, gains[1], grad_joined[:, patch:])
    grad_latents = grad_attended + grad_latent
    sums = sum_small(jnp.stack([gain_zero, gain_one, gain_two, bias_zero, bias_one, bias_two]))
    place = lax.axis_index("gx") * devices_y + lax.axis_index("gy")
    sums = lax.dynamic_slice_in_dim(sums, place * shard, shard, axis=1)
    return (
        outputs, grad_media, grad_latents, grad_query, grad_key, grad_value, grad_out.T, grad_up, grad_down.T,
        sums[:3], sums[3:],
    )


def solution(mesh):
    split = ("gx", "gy")
    images, first, second = P(split, None, None), P(split, None), P(None, split)
    return jax.shard_map(
        local,
        mesh=mesh,
        in_specs=(images, images, images, P(split), first, first, first, second, first, second, second, second),
        out_specs=(images, images, images, first, first, first, second, first, second, second, second),
        check_vma=False,
    )
```

```python
import functools
import math

import jax
import jax.numpy as jnp
from jax import lax
from jax.experimental import pallas as pl
from jax.experimental.pallas import tpu as pltpu
from jax.sharding import PartitionSpec as P

HEAD = 96
EPSILON = 1e-05
BF16 = jnp.bfloat16
F32 = jnp.float32
VMEM = 56 * 2**20
LITTLE = pl.CostEstimate(flops=1024, bytes_accessed=1024, transcendentals=0)


def product(left, right):
    return jnp.dot(left, right, preferred_element_type=F32)


def product_left(left, right):
    return lax.dot_general(left, right, (((0,), (0,)), ((), ())), preferred_element_type=F32)


def product_right(left, right):
    return lax.dot_general(left, right, (((1,), (1,)), ((), ())), preferred_element_type=F32)


def tie(*values):
    return lax.optimization_barrier(values)


def swap(block, mask, axis="gy"):
    count = lax.axis_size(axis)
    return lax.ppermute(block, axis, [(i, i ^ mask) for i in range(count)])


def far_masks():
    return [mask for mask in range(lax.axis_size("gy")) if mask % 2 == 0]


def spread(block):
    return {mask: swap(block, mask) if mask else block for mask in far_masks()}


def regroup_kernel(*refs):
    first_ref, *from_refs, to_ref = refs
    cols = from_refs[0].shape[1] // to_ref.shape[0]
    extra = first_ref.shape[0]
    for device in range(to_ref.shape[0]):
        to_ref[device, :extra] = first_ref[...]
        to_ref[device, extra:] = jnp.concatenate(
            [from_ref[:, device * cols : (device + 1) * cols] for from_ref in from_refs], axis=1
        )


def regroup(first, devices, *weights):
    shard, width = weights[0].shape
    return pl.pallas_call(
        regroup_kernel,
        out_shape=jax.ShapeDtypeStruct((devices, first.shape[0] + shard, first.shape[1]), BF16),
        compiler_params=pltpu.CompilerParams(vmem_limit_bytes=VMEM),
        cost_estimate=LITTLE,
    )(first, *weights)


def ungroup_kernel(from_ref, *to_refs):
    devices, _, width = from_ref.shape
    cols = width // len(to_refs)
    for index, to_ref in enumerate(to_refs):
        to_ref[...] = jnp.concatenate(
            [from_ref[device, :, index * cols : (index + 1) * cols] for device in range(devices)], axis=1
        ).astype(F32)


def ungroup(blocks, count):
    devices, shard, width = blocks.shape
    return pl.pallas_call(
        ungroup_kernel,
        out_shape=[jax.ShapeDtypeStruct((shard, devices * width // count), F32)] * count,
        compiler_params=pltpu.CompilerParams(vmem_limit_bytes=VMEM),
        cost_estimate=LITTLE,
    )(blocks)


def bits_of(count):
    bits, bit = [], 1
    while bit < count:
        bits.append(bit)
        bit *= 2
    return bits


def gather_small(rows, axis):
    place = lax.axis_index(axis)
    for bit in bits_of(lax.axis_size(axis)):
        other = swap(rows, bit, axis)
        upper = (place & bit) != 0
        rows = jnp.concatenate([jnp.where(upper, other, rows), jnp.where(upper, rows, other)])
    return rows


def sum_small(rows, axis):
    for bit in bits_of(lax.axis_size(axis)):
        rows = rows + swap(rows, bit, axis)
    return rows


def normed(rows, gain, bias):
    average = jnp.mean(rows, axis=-1, keepdims=True)
    centred = rows - average
    spread_of = jnp.mean(centred * centred, axis=-1, keepdims=True)
    return centred * lax.rsqrt(spread_of + EPSILON) * gain + bias


def head_mask(rows, lanes, start):
    lane = lax.broadcasted_iota(jnp.int32, (rows, lanes), 1)
    return (lane >= start) & (lane < start + HEAD)


def stacked(rows, heads, start):
    count, lanes = rows.shape
    return jnp.concatenate(
        [jnp.where(head_mask(count, lanes, start + h * HEAD), rows, jnp.zeros_like(rows)) for h in range(heads)]
    )


def unstacked(rows, heads, start):
    count, lanes = rows.shape[0] // heads, rows.shape[1]
    total = jnp.zeros((count, lanes), rows.dtype)
    for h in range(heads):
        total = jnp.where(head_mask(count, lanes, start + h * HEAD), rows[h * count : (h + 1) * count], total)
    return total


def softmax_rows(scores):
    top = jnp.max(scores, axis=-1, keepdims=True)
    raised = jnp.exp(scores - top)
    return raised / jnp.sum(raised, axis=-1, keepdims=True)


def norm_kernel(patch, rows, raw_ref, small_ref, *refs):
    joined_ref = refs[-1]
    media = normed(raw_ref[0, :patch].astype(F32), small_ref[0, 0:1], small_ref[1, 0:1])
    latent = normed(raw_ref[0, patch:rows].astype(F32), small_ref[0, 1:2], small_ref[1, 1:2])
    joined_ref[0, :patch] = media.astype(BF16)
    joined_ref[0, patch:] = latent.astype(BF16)


def norm_rows(slot, raw, small, patch, rows, total, carried):
    width = raw.shape[2]
    given = [] if carried is None else [carried]
    return pl.pallas_call(
        functools.partial(norm_kernel, patch, rows),
        grid=(1,),
        in_specs=[pl.BlockSpec(raw.shape, lambda i: (0, 0, 0)), pl.BlockSpec(small.shape, lambda i: (0, 0, 0))]
        + [pl.BlockSpec(memory_space=pl.ANY)] * len(given),
        out_specs=pl.BlockSpec((1, rows, width), lambda i: (slot, 0, 0)),
        out_shape=jax.ShapeDtypeStruct((total, rows, width), BF16),
        input_output_aliases={2 + i: i for i in range(len(given))},
        compiler_params=pltpu.CompilerParams(vmem_limit_bytes=VMEM),
        cost_estimate=LITTLE,
    )(raw, small, *given)


def attend_kernel(heads, patch, scale, given, joined_ref, mine_ref, theirs_ref, *refs):
    kv_ref, qm_ref, *out_refs = refs[given:]
    cols = mine_ref.shape[1] // 2
    count, rows, width = joined_ref.shape
    lat = rows - patch
    joined = joined_ref[...].reshape(count * rows, width)
    latent = joined_ref[:, patch:].reshape(count * lat, width)
    total = None
    for index, weights_ref in enumerate((mine_ref, theirs_ref)):
        place = slice(index * cols, (index + 1) * cols)
        kv = product(joined, weights_ref[:, :cols]).astype(BF16).reshape(count, rows, cols)
        query = (product(latent, weights_ref[:, cols:]) * scale).astype(BF16).reshape(count, lat, cols)
        kv_ref[:, :, place] = kv
        mixed = []
        for image in range(count):
            probs = softmax_rows(product_right(stacked(query[image], heads, 0), kv[image]))
            mixed.append(unstacked(product(probs.astype(BF16), kv[image]), heads, heads * HEAD).astype(BF16))
        mixed = jnp.concatenate(mixed)
        lane = lax.broadcasted_iota(jnp.int32, mixed.shape, 1)
        qm = jnp.where(lane < heads * HEAD, query.reshape(count * lat, cols), mixed)
        qm_ref[:, :, place] = qm.reshape(count, lat, cols)
        term = product_right(mixed, weights_ref[:, cols:])
        total = term if total is None else total + term
    total = total.astype(BF16).reshape(count, lat, width)
    for index, out_ref in enumerate(out_refs):

        @pl.when(pl.program_id(0) == index // count)
        def _(out_ref=out_ref, image=index % count):
            out_ref[0] = total[image]


def attend(joined, mine, theirs, heads, patch, first, steps, per, carried):
    total, rows, width = joined.shape
    lat, cols = rows - patch, mine.shape[1]
    whole = lambda shape: pl.BlockSpec(shape, lambda i: (0,) * len(shape))
    part = lambda *shape: pl.BlockSpec((per,) + shape, lambda i: (i + first, 0, 0))
    given = list(carried or ())
    return pl.pallas_call(
        functools.partial(attend_kernel, heads, patch, HEAD ** (-0.5), len(given)),
        grid=(steps,),
        in_specs=[part(rows, width), whole(mine.shape), whole(theirs.shape)]
        + [pl.BlockSpec(memory_space=pl.ANY)] * len(given),
        out_specs=[part(rows, cols), part(lat, cols)] + [whole((1, lat, width))] * (steps * per),
        out_shape=[
            jax.ShapeDtypeStruct((total, rows, cols), BF16),
            jax.ShapeDtypeStruct((total, lat, cols), BF16),
        ]
        + [jax.ShapeDtypeStruct((1, lat, width), BF16)] * (steps * per),
        input_output_aliases={3 + i: i for i in range(len(given))},
        compiler_params=pltpu.CompilerParams(vmem_limit_bytes=VMEM),
        cost_estimate=LITTLE,
    )(joined, mine, theirs, *given)


def attend_back_kernel(heads, patch, scale, given, branch_ref, kv_ref, qm_ref, mine_ref, theirs_ref, *refs):
    dkv_ref, dquery_ref, *back_refs = refs[given:]
    cols = mine_ref.shape[1] // 2
    count, lat, width = branch_ref.shape
    rows = kv_ref.shape[1]
    branch = branch_ref[...].reshape(count * lat, width)
    back, extra = None, None
    for index, weights_ref in enumerate((mine_ref, theirs_ref)):
        place = slice(index * cols, (index + 1) * cols)
        all_mixed = product(branch, weights_ref[:, cols:]).astype(BF16)
        for image in range(count):
            kv = kv_ref[image, :, place]
            query = stacked(qm_ref[image, :, place], heads, 0)
            probs = softmax_rows(product_right(query, kv))
            grad_mixed = stacked(all_mixed[image * lat : (image + 1) * lat], heads, heads * HEAD)
            grad_probs = product_right(grad_mixed, kv)
            inner = jnp.sum(grad_probs * probs, axis=-1, keepdims=True)
            grad_scores = (probs * (grad_probs - inner)).astype(BF16)
            dquery_ref[image, :, place] = unstacked(product(grad_scores, kv), heads, 0).astype(BF16)
            dkv_ref[image, :, place] = product_left(
                jnp.concatenate([grad_scores, probs.astype(BF16)]), jnp.concatenate([query, grad_mixed])
            ).astype(BF16)
        term = product_right(dkv_ref[:, :, place].reshape(count * rows, cols), weights_ref[:, :cols])
        more = product_right(dquery_ref[:, :, place].reshape(count * lat, cols), weights_ref[:, cols:]) * scale
        back = term if back is None else back + term
        extra = more if extra is None else extra + more
    back = back.reshape(count, rows, width)
    extra = extra.reshape(count, lat, width)
    for index, back_ref in enumerate(back_refs):

        @pl.when(pl.program_id(0) == index // count)
        def _(back_ref=back_ref, image=index % count):
            back_ref[0, :patch] = back[image, :patch].astype(BF16)
            back_ref[0, patch:] = (back[image, patch:] + extra[image]).astype(BF16)


def attend_back(first, steps, per, branch, kv, qm, mine, theirs, heads, patch, carried):
    total, rows, cols = kv.shape
    lat, width = branch.shape[1:]
    whole = lambda shape: pl.BlockSpec(shape, lambda i: (0,) * len(shape))
    part = lambda *shape: pl.BlockSpec((per,) + shape, lambda i: (first - i, 0, 0))
    given = list(carried or ())
    return pl.pallas_call(
        functools.partial(attend_back_kernel, heads, patch, HEAD ** (-0.5), len(given)),
        grid=(steps,),
        in_specs=[part(lat, width), part(rows, cols), part(lat, cols), whole(mine.shape), whole(theirs.shape)]
        + [pl.BlockSpec(memory_space=pl.ANY)] * len(given),
        out_specs=[part(rows, cols), part(lat, cols)] + [whole((1, rows, width))] * (steps * per),
        out_shape=[
            jax.ShapeDtypeStruct((total, rows, cols), BF16),
            jax.ShapeDtypeStruct((total, lat, cols), BF16),
        ]
        + [jax.ShapeDtypeStruct((1, rows, width), BF16)] * (steps * per),
        input_output_aliases={5 + i: i for i in range(len(given))},
        compiler_params=pltpu.CompilerParams(vmem_limit_bytes=VMEM),
        cost_estimate=LITTLE,
    )(branch, kv, qm, mine, theirs, *given)


def feed_kernel(tile, hidden_ref, cot_ref, mine_ref, theirs_ref, active_ref, upper_ref, *refs):
    *part_refs, total_ref = refs
    half = mine_ref.shape[1] // 2
    hidden, cot = hidden_ref[...], cot_ref[...]
    for index, weights_ref in enumerate((mine_ref, theirs_ref)):
        for start in range(0, half, tile):
            up = weights_ref[:, start : start + tile]
            down = weights_ref[:, half + start : half + start + tile]
            upper = product(hidden, up)
            cdf = 0.5 * (1.0 + lax.erf(upper * (0.5**0.5)))
            slope = cdf + upper * jnp.exp(-0.5 * upper * upper) * (0.5 / math.pi) ** 0.5
            grad_upper = (slope * product(cot, down)).astype(BF16)
            place = slice(index * half + start, index * half + start + tile)
            active_ref[:, place] = (upper * cdf).astype(BF16)
            upper_ref[:, place] = grad_upper
            term = product_right(grad_upper, up)
            if index == 0 and start == 0:
                total_ref[...] = term
            else:
                total_ref[...] += term
    rows = part_refs[0].shape[0]
    for index, part_ref in enumerate(part_refs):
        part_ref[...] = total_ref[index * rows : (index + 1) * rows].astype(BF16)


def feed(hidden, cot, mine, theirs, parts):
    rows, width = hidden.shape
    cols = mine.shape[1]
    whole = lambda shape: pl.BlockSpec(shape, lambda i: (0,) * len(shape))
    return pl.pallas_call(
        functools.partial(feed_kernel, math.gcd(cols // 2, 384)),
        grid=(1,),
        in_specs=[whole(hidden.shape), whole(cot.shape), whole(mine.shape), whole(theirs.shape)],
        out_specs=[whole((rows, cols))] * 2 + [whole((rows // parts, width))] * parts,
        out_shape=[jax.ShapeDtypeStruct((rows, cols), BF16)] * 2
        + [jax.ShapeDtypeStruct((rows // parts, width), BF16)] * parts,
        scratch_shapes=[pltpu.VMEM((rows, width), F32)],
        compiler_params=pltpu.CompilerParams(vmem_limit_bytes=VMEM),
        cost_estimate=LITTLE,
    )(hidden, cot, mine, theirs)


def feed_grads_kernel(hidden_ref, cot_ref, upper_ref, active_ref, *refs):
    *given_ref, to_ref = refs
    half = upper_ref.shape[1]
    for index, (left_ref, right_ref) in enumerate(((hidden_ref, upper_ref), (cot_ref, active_ref))):
        place = slice(index * half, (index + 1) * half)
        term = product_left(left_ref[...], right_ref[...])
        if given_ref:
            term = term + given_ref[0][:, place].astype(F32)
        to_ref[:, place] = term.astype(BF16)


def row_tiles(width):
    return width // math.gcd(width, 384)


def feed_grads(hidden, cot, upper, active, which, given=None):
    rows, width = hidden.shape
    half = upper.shape[1] // 2
    steps = row_tiles(width)
    left = pl.BlockSpec((rows, width // steps), lambda i: (0, i))
    right = pl.BlockSpec((rows, half), lambda i: (0, which))
    tile = pl.BlockSpec((width // steps, 2 * half), lambda i: (i, 0))
    more = [] if given is None else [given]
    return pl.pallas_call(
        feed_grads_kernel,
        grid=(steps,),
        in_specs=[left, left, right, right] + [tile] * len(more),
        out_specs=tile,
        out_shape=jax.ShapeDtypeStruct((width, 2 * half), BF16),
        compiler_params=pltpu.CompilerParams(vmem_limit_bytes=VMEM),
        cost_estimate=LITTLE,
    )(hidden, cot, upper, active, *more)


def attend_grads_kernel(heads, patch, scale, which, joined_ref, branch_ref, dkv_ref, dquery_ref, qm_ref, *refs):
    *given_refs, kv_ref, qo_ref = refs
    count, rows, tile = joined_ref.shape
    cols = kv_ref.shape[1]
    place = slice(which * cols, (which + 1) * cols)
    joined = joined_ref[...].reshape(count * rows, tile)
    latent = joined_ref[:, patch:].reshape(count * (rows - patch), tile)
    kv = product_left(joined, dkv_ref[:, :, place].reshape(count * rows, cols))
    query = product_left(latent, dquery_ref[:, :, place].reshape(latent.shape[0], cols)) * scale
    out = product_left(branch_ref[...], qm_ref[:, :, place].reshape(latent.shape[0], cols))
    lane = lax.broadcasted_iota(jnp.int32, out.shape, 1)
    qo = jnp.where(lane < heads * HEAD, query, out)
    if given_refs:
        kv = kv + given_refs[0][...].astype(F32)
        qo = qo + given_refs[1][...].astype(F32)
    kv_ref[...] = kv.astype(BF16)
    qo_ref[...] = qo.astype(BF16)


def attend_grads(joined, branch, dkv, dquery, qm, heads, patch, which, given=()):
    total, rows, width = joined.shape
    lat, cols = rows - patch, dkv.shape[2] // 2
    steps = row_tiles(width)
    half = lambda count: pl.BlockSpec((total, count, 2 * cols), lambda i: (0, 0, 0))
    tile = pl.BlockSpec((width // steps, cols), lambda i: (i, 0))
    return pl.pallas_call(
        functools.partial(attend_grads_kernel, heads, patch, HEAD ** (-0.5), which),
        grid=(steps,),
        in_specs=[
            pl.BlockSpec((total, rows, width // steps), lambda i: (0, 0, i)),
            pl.BlockSpec((total * lat, width // steps), lambda i: (0, i)),
            half(rows), half(lat), half(lat),
        ]
        + [tile] * len(given),
        out_specs=[tile] * 2,
        out_shape=[jax.ShapeDtypeStruct((width, cols), BF16)] * 2,
        compiler_params=pltpu.CompilerParams(vmem_limit_bytes=VMEM),
        cost_estimate=LITTLE,
    )(joined, branch, dkv, dquery, qm, *given)


def norm_back(rows, gain, grad):
    average = jnp.mean(rows, axis=-1, keepdims=True)
    centred = rows - average
    inverse = lax.rsqrt(jnp.mean(centred * centred, axis=-1, keepdims=True) + EPSILON)
    unit = centred * inverse
    scaled = grad * gain
    first = jnp.mean(scaled, axis=-1, keepdims=True)
    second = jnp.mean(scaled * unit, axis=-1, keepdims=True)
    back = inverse * (scaled - first - unit * second)
    axes = tuple(range(rows.ndim - 1))
    return back, jnp.sum(grad * unit, axis=axes), jnp.sum(grad, axis=axes)


def in_thirds(values):
    parts, rest = [], values
    for _ in range(3):
        part = lax.reduce_precision(rest, exponent_bits=8, mantissa_bits=7)
        parts.append(part.astype(BF16))
        rest = rest - part
    return jnp.stack(parts)


def local(media_features, latents, cotangent, image_counts, w_query, w_key, w_value, w_out, w_up, w_down,
          norm_gains, norm_biases):
    devices_x, devices_y = lax.axis_size("gx"), lax.axis_size("gy")
    masks = far_masks()
    img_count, lat, width = latents.shape
    patch = media_features.shape[1]
    rows = patch + lat
    shard = w_query.shape[0]
    head_width = width // devices_y
    heads = head_width // HEAD
    ff_width = w_up.shape[1] // devices_y
    total = img_count * len(masks)

    four_width = 4 * head_width
    small = in_thirds(jnp.stack([norm_gains, norm_biases])).reshape(-1)
    extra = -(-small.size // (16 * four_width)) * 16
    small = jnp.pad(small, (0, extra * four_width - small.size)).reshape(extra, four_width)
    four = regroup(small, devices_y, w_key, w_value, w_query, w_out.T)
    four = lax.all_to_all(four, "gy", split_axis=0, concat_axis=0, tiled=True)
    mine = lax.all_gather(four[:, extra:].reshape(devices_y * shard, four_width), "gx", axis=0, tiled=True)

    two = jnp.concatenate(
        [part.reshape(shard, devices_y, ff_width).transpose(1, 0, 2) for part in (w_up, w_down.T)], axis=2
    )
    two, four = tie(two, four)
    small = four[:, :extra].reshape(devices_y, -1)[:, : 18 * shard].reshape(devices_y, 3, 6 * shard)
    small = gather_small(jnp.sum(small.astype(F32), axis=1).reshape(1, -1), "gx")
    small = small.reshape(devices_x, devices_y, 6, shard).transpose(2, 0, 1, 3).reshape(2, 3, width)

    two = lax.all_to_all(two, "gy", split_axis=0, concat_axis=0, tiled=True)
    live = (jnp.arange(img_count, dtype=jnp.int32) < image_counts[0]).astype(BF16)
    cot_own = cotangent * live[:, None, None]
    own = [
        jnp.concatenate([part[i : i + 1] for part in (media_features, latents, cot_own)], axis=1) for i in range(img_count)
    ]
    two, small, *own = tie(two, small, *own)
    ff_rows = two.reshape(devices_y * shard, 2 * ff_width)
    gains, biases = small[0], small[1]

    raw = {(0, i): own[i] for i in range(img_count)}
    joined_all = None
    if len(masks) == 4 and img_count == 2:
        slots = [(0, 0), (0, 1), (2, 0), (4, 0), (2, 1), (4, 1), (6, 0), (6, 1)]
        batches = (2, 1, 1)
        for slot in range(2):
            joined_all = norm_rows(slot, raw[slots[slot]], small, patch, rows, total, joined_all)
        raw[2, 0], raw[4, 0], ff_rows, later, joined_all = tie(
            swap(own[0], 2), swap(own[0], 4), ff_rows, own[1], joined_all
        )
        raw[2, 1], raw[4, 1], raw[6, 0] = swap(later, 2), swap(later, 4), swap(raw[2, 0], 4)
        raw[6, 1] = swap(raw[4, 1], 2)
    else:
        slots = [(mask, i) for mask in masks for i in range(img_count)]
        batches = (total // img_count - 1, 1)
        for mask in masks[1:]:
            raw.update({(mask, i): swap(own[i], mask) for i in range(img_count)})
    ff_mine = lax.all_gather(ff_rows, "gx", axis=0, tiled=True)
    theirs = swap(mine, 1)

    carried, out_parts, step = None, {}, 0
    for count in batches:
        here = range(step * img_count, (step + count) * img_count)
        if carried:
            joined_all, carried[0], *arrived = tie(joined_all, carried[0], *[raw[slots[slot]] for slot in here])
            raw.update({slots[slot]: part for slot, part in zip(here, arrived)})
        for slot in here:
            if slots[slot][0] or len(masks) != 4:
                joined_all = norm_rows(slot, raw[slots[slot]], small, patch, rows, total, joined_all)
        kv_all, qm_all, *parts = attend(joined_all, mine, theirs, heads, patch, step, count, img_count, carried)
        carried = [kv_all, qm_all]
        out_parts.update({slots[slot]: part for slot, part in zip(here, parts)})
        step += count

    def collect(parts):
        return jnp.concatenate(
            [
                sum(swap(parts[mask, i], mask).astype(F32) if mask else parts[mask, i].astype(F32) for mask in masks)
                for i in range(img_count)
            ]
        )

    cot_all = jnp.concatenate([raw[mask, i][:, rows:] for mask in masks for i in range(img_count)]).reshape(-1, width)
    latent_float = latents.astype(F32)
    attended = collect(out_parts) + latent_float
    hidden_own = normed(attended, gains[2], biases[2]).astype(BF16)
    *hidden, ff_mine = tie(*spread(hidden_own).values(), ff_mine)
    ff_theirs = swap(ff_mine, 1)
    hidden = jnp.concatenate(hidden).reshape(-1, width)

    def collect_pairs(parts):
        parts = [part.reshape(img_count, lat, width) for part in parts]
        return [parts[0]] + [swap(part, mask) for mask, part in zip(masks[1:], parts[1:])]

    total_of = lambda parts: sum(part.astype(F32) for part in parts)

    active, grad_upper, *hidden_parts = feed(hidden, cot_all, ff_mine, ff_theirs, len(masks))
    ff_operands = hidden, cot_all, grad_upper, active
    given = swap(feed_grads(*ff_operands, 1), 1)
    *hidden_parts, given = tie(*collect_pairs(hidden_parts), given)
    grad_norm_input, gain_two, bias_two = norm_back(attended, gains[2], total_of(hidden_parts))
    grad_attended = cot_own.astype(F32) + grad_norm_input
    grad_branch, given = tie(grad_attended.astype(BF16), given)
    branch = spread(grad_branch)
    ff_grads = feed_grads(*ff_operands, 0, given)
    ff_part = lax.psum_scatter(ff_grads, "gx", scatter_dimension=0, tiled=True)
    ffn_parts = product_right(active[:, :ff_width], ff_mine[:, ff_width:]) + product_right(
        active[:, ff_width:], ff_theirs[:, ff_width:]
    )
    *branch, ffn_parts, _ = tie(*branch.values(), ffn_parts.astype(BF16), ff_grads)
    branch = jnp.concatenate([branch[masks.index(mask)][i : i + 1] for mask, i in slots])

    steps = total // img_count
    arrays = branch, kv_all, qm_all, mine, theirs, heads, patch
    *carried, last, last_but_one = attend_back(steps - 1, 1, img_count, *arrays, None)
    dkv_all, dquery_all, *back = attend_back(steps - 2, steps - 1, img_count, *arrays, carried)
    back = [part for step in range(steps - 1) for part in back[step * img_count : (step + 1) * img_count]]
    order = [slots[step * img_count + i] for step in reversed(range(steps)) for i in range(img_count)]
    back = dict(zip(order, [last, last_but_one, *back]))

    def plus(left, right):
        return (left.astype(F32) + right.astype(F32)).astype(BF16)

    if len(masks) == 4 and img_count == 2:
        through = plus(back[2, 0], swap(back[6, 0], 4)), plus(back[4, 1], swap(back[6, 1], 2))
        dkv_all, dquery_all, *through = tie(dkv_all, dquery_all, *through)
        arrived = [
            back[0, 0], swap(through[0], 2), swap(back[4, 0], 4),
            back[0, 1], swap(back[2, 1], 2), swap(through[1], 4),
        ]
    else:
        arrived = [swap(back[mask, i], mask) if mask else back[mask, i] for i in range(img_count) for mask in masks]

    at_operands = joined_all, branch.reshape(total * lat, width), dkv_all, dquery_all, qm_all, heads, patch
    given = [swap(part, 1) for part in attend_grads(*at_operands, 1)]
    at_grads = attend_grads(*at_operands, 0, given)
    early, late = (lax.all_to_all(part, "gx", split_axis=0, concat_axis=0, tiled=True) for part in at_grads)
    *arrived, early, ff_part, ffn_parts = tie(*arrived, early, ff_part, ffn_parts)
    each = len(arrived) // img_count
    grad_joined = jnp.concatenate([total_of(arrived[i * each : (i + 1) * each]) for i in range(img_count)])

    grad_media, gain_zero, bias_zero = norm_back(media_features.astype(F32), gains[0], grad_joined[:, :patch])
    grad_latent, gain_one, bias_one = norm_back(latent_float, gains[1], grad_joined[:, patch:])
    grad_latents = grad_attended + grad_latent
    sums = sum_small(jnp.stack([gain_zero, gain_one, gain_two, bias_zero, bias_one, bias_two]), "gy")

    def home(part):
        return lax.all_to_all(part.reshape(devices_y, shard, -1), "gy", split_axis=0, concat_axis=0, tiled=True)

    result = attended + total_of(collect_pairs(ffn_parts.reshape(len(masks), img_count * lat, width)))
    outputs = (result * live.astype(F32)[:, None, None]).astype(BF16)
    grad_up, grad_down = ungroup(home(ff_part), 2)
    grad_down = grad_down.T
    late, sums, grad_up, grad_down, outputs, grad_media = tie(late, sums, grad_up, grad_down, outputs, grad_media)
    sums = sum_small(sums, "gx")
    place = lax.axis_index("gx") * devices_y + lax.axis_index("gy")
    sums = lax.dynamic_slice_in_dim(sums, place * shard, shard, axis=1)
    shares = jnp.concatenate(
        [
            jnp.sum(part.reshape(devices_x, devices_y * shard, 2 * head_width).astype(F32), axis=0)
            for part in (early, late)
        ],
        axis=1,
    )
    grad_key, grad_value, grad_query, grad_out = ungroup(home(shares.astype(BF16)), 4)
    return (
        outputs, grad_media, grad_latents, grad_query, grad_key, grad_value, grad_out.T, grad_up, grad_down,
        sums[:3], sums[3:],
    )


def solution(mesh):
    split = ("gx", "gy")
    images, first, second = P(split, None, None), P(split, None), P(None, split)
    return jax.shard_map(
        local,
        mesh=mesh,
        in_specs=(images, images, images, P(split), first, first, first, second, first, second, second, second),
        out_specs=(images, images, images, first, first, first, second, first, second, second, second),
        check_vma=False,
    )
```

```python
import functools
import math

import jax
import jax.numpy as jnp
from jax import lax
from jax.experimental import pallas as pl
from jax.experimental.pallas import tpu as pltpu
from jax.sharding import PartitionSpec as P

HEAD = 96
EPSILON = 1e-05
BF16 = jnp.bfloat16
F32 = jnp.float32
VMEM = 56 * 2**20
LITTLE = pl.CostEstimate(flops=1024, bytes_accessed=1024, transcendentals=0)


def product(left, right):
    return jnp.dot(left, right, preferred_element_type=F32)


def product_left(left, right):
    return lax.dot_general(left, right, (((0,), (0,)), ((), ())), preferred_element_type=F32)


def product_right(left, right):
    return lax.dot_general(left, right, (((1,), (1,)), ((), ())), preferred_element_type=F32)


def tie(*values):
    return lax.optimization_barrier(values)


def swap(block, mask, axis="gy"):
    count = lax.axis_size(axis)
    return lax.ppermute(block, axis, [(i, i ^ mask) for i in range(count)])


def far_masks():
    return [mask for mask in range(lax.axis_size("gy")) if mask % 2 == 0]


def spread(block):
    return {mask: swap(block, mask) if mask else block for mask in far_masks()}


def regroup_kernel(first_ref, *refs):
    *from_refs, to_ref = refs
    extra, half = first_ref.shape[0], len(from_refs) // 2
    groups = to_ref.shape[0] // 2
    cols = from_refs[0].shape[1] // groups
    for device in range(2 * groups):
        group, core = device // 2, device % 2
        to_ref[device, :extra] = first_ref[...]
        for index, from_ref in enumerate(from_refs[core * half : (core + 1) * half]):
            to_ref[device, extra:, index * cols : (index + 1) * cols] = from_ref[:, group * cols : (group + 1) * cols]


def regroup(first, devices, *weights):
    shard, width = weights[0].shape
    return pl.pallas_call(
        regroup_kernel,
        out_shape=jax.ShapeDtypeStruct((devices, first.shape[0] + shard, first.shape[1]), BF16),
        compiler_params=pltpu.CompilerParams(vmem_limit_bytes=VMEM),
        cost_estimate=LITTLE,
    )(first, *weights)


def ungroup_kernel(by_pair, from_ref, *to_refs):
    devices, _, width = from_ref.shape
    per = len(to_refs) // 2 if by_pair else len(to_refs)
    cols = width // per
    for index, to_ref in enumerate(to_refs):
        sources = range(index // per, devices, 2) if by_pair else range(devices)
        place = slice(index % per * cols, (index % per + 1) * cols)
        for position, device in enumerate(sources):
            to_ref[:, position * cols : (position + 1) * cols] = from_ref[device, :, place].astype(F32)


def ungroup(blocks, count, by_pair):
    devices, shard, width = blocks.shape
    return pl.pallas_call(
        functools.partial(ungroup_kernel, by_pair),
        out_shape=[jax.ShapeDtypeStruct((shard, devices * width // count), F32)] * count,
        compiler_params=pltpu.CompilerParams(vmem_limit_bytes=VMEM),
        cost_estimate=LITTLE,
    )(blocks)


def bits_of(count):
    bits, bit = [], 1
    while bit < count:
        bits.append(bit)
        bit *= 2
    return bits


def gather_small(rows, axis):
    place = lax.axis_index(axis)
    for bit in bits_of(lax.axis_size(axis)):
        other = swap(rows, bit, axis)
        upper = (place & bit) != 0
        rows = jnp.concatenate([jnp.where(upper, other, rows), jnp.where(upper, rows, other)])
    return rows


def sum_small(rows):
    rows = rows + swap(rows, 1)
    rows = sum([rows] + [swap(rows, mask) for mask in far_masks()[1:]])
    return sum([rows] + [swap(rows, mask, "gx") for mask in range(1, lax.axis_size("gx"))])


def normed(rows, gain, bias):
    average = jnp.mean(rows, axis=-1, keepdims=True)
    centred = rows - average
    spread_of = jnp.mean(centred * centred, axis=-1, keepdims=True)
    return centred * lax.rsqrt(spread_of + EPSILON) * gain + bias


def head_mask(rows, lanes, head):
    lane = lax.broadcasted_iota(jnp.int32, (rows, lanes), 1)
    return (lane >= head * HEAD) & (lane < (head + 1) * HEAD)


def stacked(rows, heads):
    count, lanes = rows.shape
    return jnp.concatenate(
        [jnp.where(head_mask(count, lanes, h), rows, jnp.zeros_like(rows)) for h in range(heads)]
    )


def unstacked(rows, heads):
    count, lanes = rows.shape[0] // heads, rows.shape[1]
    total = rows[:count]
    for h in range(1, heads):
        total = jnp.where(head_mask(count, lanes, h), rows[h * count : (h + 1) * count], total)
    return total


def softmax_rows(scores):
    top = jnp.max(scores, axis=-1, keepdims=True)
    raised = jnp.exp(scores - top)
    return raised / jnp.sum(raised, axis=-1, keepdims=True)


def load_weights(pair_ref, mine_ref, theirs_ref, kv_weights, qo_weights, sems):
    @pl.when(pair_ref[0] == 0)
    def _():
        pltpu.make_async_copy(mine_ref, kv_weights, sems.at[0]).start()
        pltpu.make_async_copy(theirs_ref, qo_weights, sems.at[1]).start()

    @pl.when(pair_ref[0] == 1)
    def _():
        pltpu.make_async_copy(theirs_ref, kv_weights, sems.at[0]).start()
        pltpu.make_async_copy(mine_ref, qo_weights, sems.at[1]).start()

    return [
        pltpu.make_async_copy(mine_ref, kv_weights, sems.at[0]),
        pltpu.make_async_copy(theirs_ref, qo_weights, sems.at[1]),
    ]


def attend_kernel(heads, patch, scale, raws, given, pair_ref, mine_ref, theirs_ref, small_ref, *refs):
    *refs, kv_weights, qo_weights, sems = refs
    joined_ref, kv_ref, qm_ref, *out_refs = refs[raws + given :]
    count, rows, width = joined_ref.shape
    copies = load_weights(pair_ref, mine_ref, theirs_ref, kv_weights, qo_weights, sems)
    for image, raw_ref in enumerate(refs[:raws]):
        media = normed(raw_ref[0, :patch].astype(F32), small_ref[0, 0:1], small_ref[1, 0:1])
        latent = normed(raw_ref[0, patch:rows].astype(F32), small_ref[0, 1:2], small_ref[1, 1:2])
        joined_ref[image, :patch] = media.astype(BF16)
        joined_ref[image, patch:] = latent.astype(BF16)
    for copy in copies:
        copy.wait()
    lat, cols = rows - patch, kv_weights.shape[1] // 2
    joined = joined_ref[...].reshape(count * rows, width)
    latent = joined_ref[:, patch:].reshape(count * lat, width)
    kv_ref[...] = product(joined, kv_weights[...]).astype(BF16).reshape(count, rows, 2 * cols)
    query = (product(latent, qo_weights[:, :cols]) * scale).astype(BF16)
    qm_ref[:, :, :cols] = query.reshape(count, lat, cols)
    mixed = []
    for image in range(count):
        probs = softmax_rows(product_right(stacked(query[image * lat : (image + 1) * lat], heads), kv_ref[image, :, :cols]))
        mixed.append(unstacked(product(probs.astype(BF16), kv_ref[image, :, cols:]), heads).astype(BF16))
    mixed = jnp.concatenate(mixed)
    qm_ref[:, :, cols:] = mixed.reshape(count, lat, cols)
    total = product_right(mixed, qo_weights[:, cols:]).astype(BF16).reshape(count, lat, width)
    for image, out_ref in enumerate(out_refs):
        out_ref[0] = total[image]


SMALL = pl.BlockSpec(memory_space=pltpu.SMEM)
ANY = pl.BlockSpec(memory_space=pl.ANY)


def weight_scratch(mine):
    return [pltpu.VMEM(mine.shape, BF16)] * 2 + [pltpu.SemaphoreType.DMA((2,))]


def attend(pair, mine, theirs, small, raws, heads, patch, rows, step, total, carried):
    width, cols = mine.shape
    lat, per = rows - patch, len(raws)
    part = lambda *shape: pl.BlockSpec((per,) + shape, lambda i: (step, 0, 0))
    given = list(carried or ())
    return pl.pallas_call(
        functools.partial(attend_kernel, heads, patch, HEAD ** (-0.5), per, len(given)),
        grid=(1,),
        in_specs=[SMALL, ANY, ANY, whole(small.shape)] + [whole(raw.shape) for raw in raws] + [ANY] * len(given),
        out_specs=[part(rows, width), part(rows, cols), part(lat, cols)] + [whole((1, lat, width))] * per,
        out_shape=[
            jax.ShapeDtypeStruct((total, rows, width), BF16),
            jax.ShapeDtypeStruct((total, rows, cols), BF16),
            jax.ShapeDtypeStruct((total, lat, cols), BF16),
        ]
        + [jax.ShapeDtypeStruct((1, lat, width), BF16)] * per,
        scratch_shapes=weight_scratch(mine),
        input_output_aliases={4 + per + i: i for i in range(len(given))},
        compiler_params=pltpu.CompilerParams(vmem_limit_bytes=VMEM),
        cost_estimate=LITTLE,
    )(pair, mine, theirs, small, *raws, *given)


def attend_back_kernel(heads, patch, scale, given, pair_ref, mine_ref, theirs_ref, branch_ref, kv_ref, qm_ref, *refs):
    *refs, kv_weights, qo_weights, sems = refs

    @pl.when(pl.program_id(0) == 0)
    def _():
        for copy in load_weights(pair_ref, mine_ref, theirs_ref, kv_weights, qo_weights, sems):
            copy.wait()

    dkv_ref, dquery_ref, *back_refs = refs[given:]
    count, lat, width = branch_ref.shape
    rows, cols = kv_ref.shape[1], kv_ref.shape[2] // 2
    branch = branch_ref[...].reshape(count * lat, width)
    all_mixed = product(branch, qo_weights[:, cols:]).astype(BF16)
    for image in range(count):
        keys, values = kv_ref[image, :, :cols], kv_ref[image, :, cols:]
        query = stacked(qm_ref[image, :, :cols], heads)
        probs = softmax_rows(product_right(query, keys))
        grad_mixed = stacked(all_mixed[image * lat : (image + 1) * lat], heads)
        grad_probs = product_right(grad_mixed, values)
        inner = jnp.sum(grad_probs * probs, axis=-1, keepdims=True)
        grad_scores = (probs * (grad_probs - inner)).astype(BF16)
        dquery_ref[image] = unstacked(product(grad_scores, keys), heads).astype(BF16)
        dkv_ref[image, :, :cols] = product_left(grad_scores, query).astype(BF16)
        dkv_ref[image, :, cols:] = product_left(probs.astype(BF16), grad_mixed).astype(BF16)
    back = product_right(dkv_ref[...].reshape(count * rows, 2 * cols), kv_weights[...]).reshape(count, rows, width)
    extra = product_right(dquery_ref[...].reshape(count * lat, cols), qo_weights[:, :cols]) * scale
    extra = extra.reshape(count, lat, width)
    for index, back_ref in enumerate(back_refs):

        @pl.when(pl.program_id(0) == index // count)
        def _(back_ref=back_ref, image=index % count):
            back_ref[0, :patch] = back[image, :patch].astype(BF16)
            back_ref[0, patch:] = (back[image, patch:] + extra[image]).astype(BF16)


def attend_back(pair, mine, theirs, branch, kv, qm, heads, patch, first, steps, per, carried):
    total, rows, cols = kv.shape
    lat, width = branch.shape[1:]
    part = lambda *shape: pl.BlockSpec((per,) + shape, lambda i: (first - i, 0, 0))
    given = list(carried or ())
    dkv, dquery, *backs = pl.pallas_call(
        functools.partial(attend_back_kernel, heads, patch, HEAD ** (-0.5), len(given)),
        grid=(steps,),
        in_specs=[SMALL, ANY, ANY, part(lat, width), part(rows, cols), part(lat, cols)] + [ANY] * len(given),
        out_specs=[part(rows, cols), part(lat, cols // 2)] + [whole((1, rows, width))] * (steps * per),
        out_shape=[
            jax.ShapeDtypeStruct((total, rows, cols), BF16),
            jax.ShapeDtypeStruct((total, lat, cols // 2), BF16),
        ]
        + [jax.ShapeDtypeStruct((1, rows, width), BF16)] * (steps * per),
        scratch_shapes=weight_scratch(mine),
        input_output_aliases={6 + i: i for i in range(len(given))},
        compiler_params=pltpu.CompilerParams(vmem_limit_bytes=VMEM),
        cost_estimate=LITTLE,
    )(pair, mine, theirs, branch, kv, qm, *given)
    return dkv, dquery, backs


def feed_kernel(tile, parts, cot_ref, cot_other_ref, weights_ref, *refs):
    hidden_refs, refs = refs[:parts], refs[parts:]
    all_ref, cots_ref, active_ref, upper_ref, *part_refs, ups, downs, total_ref, sems = refs
    cols = weights_ref.shape[1] // 2
    copies = []
    for index, start in enumerate(range(0, cols, tile)):
        copies.append(pltpu.make_async_copy(weights_ref.at[:, pl.ds(start, tile)], ups.at[index], sems.at[0, index]))
        copies.append(
            pltpu.make_async_copy(weights_ref.at[:, pl.ds(cols + start, tile)], downs.at[index], sems.at[1, index])
        )
    for copy in copies:
        copy.start()
    start = 0
    for hidden_ref in hidden_refs:
        all_ref[start : start + hidden_ref.shape[0]] = hidden_ref[...]
        start += hidden_ref.shape[0]
    cots_ref[: start // 2] = cot_ref[...]
    cots_ref[start // 2 :] = cot_other_ref[...]
    hidden, cot = all_ref[...], cots_ref[...]
    for index in range(cols // tile):
        copies[2 * index].wait()
        copies[2 * index + 1].wait()
        up = ups[index]
        upper = product(hidden, up)
        cdf = 0.5 * (1.0 + lax.erf(upper * (0.5**0.5)))
        slope = cdf + upper * jnp.exp(-0.5 * upper * upper) * (0.5 / math.pi) ** 0.5
        grad_upper = (slope * product(cot, downs[index])).astype(BF16)
        place = slice(index * tile, (index + 1) * tile)
        active_ref[:, place] = (upper * cdf).astype(BF16)
        upper_ref[:, place] = grad_upper
        term = product_right(grad_upper, up)
        if index == 0:
            total_ref[...] = term
        else:
            total_ref[...] += term
    start = 0
    for part_ref in part_refs:
        part_ref[...] = total_ref[start : start + part_ref.shape[0]].astype(BF16)
        start += part_ref.shape[0]


def feed(hidden, cot, cot_other, weights):
    width = cot.shape[1]
    rows = 2 * cot.shape[0]
    cols = weights.shape[1] // 2
    tile = 256 if cols % 256 == 0 else math.gcd(cols, 384)
    shapes = [(rows, width)] * 2 + [(rows, cols)] * 2 + [part.shape for part in hidden]
    return pl.pallas_call(
        functools.partial(feed_kernel, tile, len(hidden)),
        grid=(1,),
        in_specs=[whole(cot.shape)] * 2 + [ANY] + [whole(part.shape) for part in hidden],
        out_specs=[whole(shape) for shape in shapes],
        out_shape=[jax.ShapeDtypeStruct(shape, BF16) for shape in shapes],
        scratch_shapes=[pltpu.VMEM((cols // tile, width, tile), BF16)] * 2
        + [pltpu.VMEM((rows, width), F32), pltpu.SemaphoreType.DMA((2, cols // tile))],
        compiler_params=pltpu.CompilerParams(vmem_limit_bytes=VMEM),
        cost_estimate=LITTLE,
    )(cot, cot_other, weights, *hidden)


def feed_out_kernel(active_ref, weights_ref, own_ref, other_ref):
    rows = own_ref.shape[0]
    own_ref[...] = product_right(active_ref[:rows], weights_ref[...]).astype(BF16)
    other_ref[...] = product_right(active_ref[rows:], weights_ref[...]).astype(BF16)


def feed_out(active, weights):
    rows, cols = active.shape
    width = weights.shape[0]
    return pl.pallas_call(
        feed_out_kernel,
        grid=(1,),
        in_specs=[whole(active.shape), pl.BlockSpec((width, cols), lambda i: (0, 1))],
        out_specs=[whole((rows // 2, width))] * 2,
        out_shape=[jax.ShapeDtypeStruct((rows // 2, width), BF16)] * 2,
        compiler_params=pltpu.CompilerParams(vmem_limit_bytes=VMEM),
        cost_estimate=LITTLE,
    )(active, weights)


def feed_grads_kernel(hidden_ref, cot_ref, upper_ref, active_ref, to_ref):
    half = upper_ref.shape[1]
    to_ref[:, :half] = product_left(hidden_ref[...], upper_ref[...]).astype(BF16)
    to_ref[:, half:] = product_left(cot_ref[...], active_ref[...]).astype(BF16)


def row_tiles(width):
    return width // math.gcd(width, 384)


def feed_grads(hidden, cot, upper, active):
    rows, width = hidden.shape
    cols = upper.shape[1]
    steps = row_tiles(width)
    left = pl.BlockSpec((rows, width // steps), lambda i: (0, i))
    right = pl.BlockSpec((rows, cols), lambda i: (0, 0))
    return pl.pallas_call(
        feed_grads_kernel,
        grid=(steps,),
        in_specs=[left, left, right, right],
        out_specs=pl.BlockSpec((width // steps, 2 * cols), lambda i: (i, 0)),
        out_shape=jax.ShapeDtypeStruct((width, 2 * cols), BF16),
        compiler_params=pltpu.CompilerParams(vmem_limit_bytes=VMEM),
        cost_estimate=LITTLE,
    )(hidden, cot, upper, active)


def add_pieces_kernel(first_ref, *refs):
    *piece_refs, to_ref = refs
    rows = piece_refs[0].shape[0]
    for index, piece_ref in enumerate(piece_refs):
        place = slice(index * rows, (index + 1) * rows)
        to_ref[place] = (first_ref[place].astype(F32) + piece_ref[...].astype(F32)).astype(BF16)


def pick_kernel(*refs):
    *from_refs, to_ref = refs
    rows = from_refs[0].shape[1]
    for index, from_ref in enumerate(from_refs):
        to_ref[index * rows : (index + 1) * rows] = from_ref[0]


def pick(parts, block, rows):
    width = parts[0].shape[2]
    return pl.pallas_call(
        pick_kernel,
        grid=(1,),
        in_specs=[pl.BlockSpec((1, rows, width), lambda i: (0, block, 0))] * len(parts),
        out_specs=pl.BlockSpec((len(parts) * rows, width), lambda i: (0, 0)),
        out_shape=jax.ShapeDtypeStruct((len(parts) * rows, width), BF16),
        compiler_params=pltpu.CompilerParams(vmem_limit_bytes=VMEM),
        cost_estimate=LITTLE,
    )(*parts)


def attend_grads_kernel(patch, scale, pair_ref, joined_ref, branch_ref, dkv_ref, dquery_ref, qm_ref, keep_ref, *give_refs):
    count, rows, tile = joined_ref.shape
    lat, cols = rows - patch, dquery_ref.shape[2]
    joined = joined_ref[...].reshape(count * rows, tile)
    latent = joined_ref[:, patch:].reshape(count * lat, tile)
    kv = product_left(joined, dkv_ref[...].reshape(count * rows, 2 * cols)).astype(BF16)
    query = (product_left(latent, dquery_ref[...].reshape(count * lat, cols)) * scale).astype(BF16)
    out = product_left(branch_ref[...], qm_ref[:, :, cols:].reshape(count * lat, cols)).astype(BF16)

    @pl.when(pair_ref[0] == 0)
    def _():
        keep_ref[...] = kv

    @pl.when(pair_ref[0] == 1)
    def _():
        keep_ref[:, :cols] = query
        keep_ref[:, cols:] = out

    for step, give_ref in enumerate(give_refs):

        @pl.when((pl.program_id(0) == step) & (pair_ref[0] == 0))
        def _(give_ref=give_ref):
            give_ref[:, :cols] = query
            give_ref[:, cols:] = out

        @pl.when((pl.program_id(0) == step) & (pair_ref[0] == 1))
        def _(give_ref=give_ref):
            give_ref[...] = kv


def attend_grads(pair, joined, branch, dkv, dquery, qm, patch):
    total, rows, width = joined.shape
    lat, cols = rows - patch, dkv.shape[2]
    steps = row_tiles(width)
    tile = pl.BlockSpec((width // steps, cols), lambda i: (i, 0))
    return pl.pallas_call(
        functools.partial(attend_grads_kernel, patch, HEAD ** (-0.5)),
        grid=(steps,),
        in_specs=[
            SMALL,
            pl.BlockSpec((total, rows, width // steps), lambda i: (0, 0, i)),
            pl.BlockSpec((total * lat, width // steps), lambda i: (0, i)),
            whole(dkv.shape), whole(dquery.shape), whole(qm.shape),
        ],
        out_specs=[tile] + [whole((width // steps, cols))] * steps,
        out_shape=[jax.ShapeDtypeStruct((width, cols), BF16)] + [jax.ShapeDtypeStruct((width // steps, cols), BF16)] * steps,
        compiler_params=pltpu.CompilerParams(vmem_limit_bytes=VMEM),
        cost_estimate=LITTLE,
    )(pair, joined, branch, dkv, dquery, qm)


def whole(shape):
    return pl.BlockSpec(shape, lambda *_: (0,) * len(shape))


def once(kernel, operands, shapes, specs=None):
    specs = specs or [whole(operand.shape) for operand in operands]
    return pl.pallas_call(
        kernel,
        grid=(1,),
        in_specs=specs,
        out_specs=[whole(shape) for shape, _ in shapes],
        out_shape=[jax.ShapeDtypeStruct(shape, kind) for shape, kind in shapes],
        compiler_params=pltpu.CompilerParams(vmem_limit_bytes=VMEM),
        cost_estimate=LITTLE,
    )(*operands)


def attended_kernel(small_ref, latent_ref, *refs):
    *part_refs, attended_ref, hidden_ref = refs
    images = latent_ref.shape[0]
    each = len(part_refs) // images
    for image in range(images):
        total = latent_ref[image].astype(F32)
        for part_ref in part_refs[image * each : (image + 1) * each]:
            total = total + part_ref[0].astype(F32)
        attended_ref[image] = total
        hidden_ref[image] = normed(total, small_ref[0, 2:3], small_ref[1, 2:3]).astype(BF16)


def summed_kernel(other_ref, *refs):
    count = len(refs) // 2
    rows = other_ref.shape[0] // count
    for index in range(count):
        other = other_ref[index * rows : (index + 1) * rows].astype(F32)
        refs[count + index][...] = (refs[index][...].astype(F32) + other).astype(BF16)


def through_kernel(*refs):
    for index in range(2):
        left_ref, right_ref, to_ref = refs[2 * index], refs[2 * index + 1], refs[4 + index]
        to_ref[...] = (left_ref[...].astype(F32) + right_ref[...].astype(F32)).astype(BF16)


def norm_back(rows, gain, grad):
    average = jnp.mean(rows, axis=-1, keepdims=True)
    centred = rows - average
    inverse = lax.rsqrt(jnp.mean(centred * centred, axis=-1, keepdims=True) + EPSILON)
    unit = centred * inverse
    scaled = grad * gain
    first = jnp.mean(scaled, axis=-1, keepdims=True)
    second = jnp.mean(scaled * unit, axis=-1, keepdims=True)
    back = inverse * (scaled - first - unit * second)
    return back, jnp.sum(grad * unit, axis=0, keepdims=True), jnp.sum(grad, axis=0, keepdims=True)


def branch_kernel(small_ref, attended_ref, cot_ref, *refs):
    *part_refs, grad_ref, branch_ref, sums_ref = refs
    images, lat, width = attended_ref.shape
    grad = sum(part_ref[...].astype(F32) for part_ref in part_refs)
    back, gain, bias = norm_back(attended_ref[...].reshape(images * lat, width), small_ref[0, 2:3], grad)
    total = (cot_ref[...].reshape(images * lat, width).astype(F32) + back).reshape(images, lat, width)
    grad_ref[...] = total
    branch_ref[...] = total.astype(BF16)
    sums_ref[0:1] = gain
    sums_ref[1:2] = bias


def rows_back_kernel(small_ref, sums_two_ref, media_ref, latent_ref, grad_ref, *refs):
    *part_refs, media_to_ref, latent_to_ref, sums_ref = refs
    images, patch, _ = media_ref.shape
    each = len(part_refs) // images
    totals = None
    for image in range(images):
        parts = part_refs[image * each : (image + 1) * each]
        grad = sum(part_ref[0, :patch].astype(F32) for part_ref in parts)
        media, gain_zero, bias_zero = norm_back(media_ref[image].astype(F32), small_ref[0, 0:1], grad)
        media_to_ref[image] = media
        grad = sum(part_ref[0, patch:].astype(F32) for part_ref in parts)
        latent, gain_one, bias_one = norm_back(latent_ref[image].astype(F32), small_ref[0, 1:2], grad)
        latent_to_ref[image] = grad_ref[image] + latent
        terms = gain_zero, gain_one, bias_zero, bias_one
        totals = terms if totals is None else [left + right for left, right in zip(totals, terms)]
    for row, total in zip((0, 1, 3, 4), totals):
        sums_ref[row : row + 1] = total
    sums_ref[2:3] = sums_two_ref[0:1]
    sums_ref[5:6] = sums_two_ref[1:2]


def in_thirds(values):
    parts, rest = [], values
    for _ in range(3):
        part = lax.reduce_precision(rest, exponent_bits=8, mantissa_bits=7)
        parts.append(part.astype(BF16))
        rest = rest - part
    return jnp.stack(parts)


def local(media_features, latents, cotangent, image_counts, w_query, w_key, w_value, w_out, w_up, w_down,
          norm_gains, norm_biases):
    devices_x, devices_y = lax.axis_size("gx"), lax.axis_size("gy")
    masks = far_masks()
    img_count, lat, width = latents.shape
    patch = media_features.shape[1]
    rows = patch + lat
    shard = w_query.shape[0]
    head_width = width // devices_y
    heads = 2 * head_width // HEAD
    pair = (lax.axis_index("gy") % 2).astype(jnp.int32).reshape(1)
    ff_width = w_up.shape[1] // devices_y
    total = img_count * len(masks)

    four_width = 4 * head_width
    small = in_thirds(jnp.stack([norm_gains, norm_biases])).reshape(-1)
    extra = -(-small.size // (16 * four_width)) * 16
    small = jnp.pad(small, (0, extra * four_width - small.size)).reshape(extra, four_width)
    four = regroup(small, devices_y, w_key, w_value, w_query, w_out.T)
    four = lax.all_to_all(four, "gy", split_axis=0, concat_axis=0, tiled=True)
    mine = lax.all_gather(four[:, extra:].reshape(devices_y * shard, four_width), "gx", axis=0, tiled=True)

    two = jnp.concatenate(
        [part.reshape(shard, devices_y, ff_width).transpose(1, 0, 2) for part in (w_up, w_down.T)], axis=2
    )
    two, four = tie(two, four)
    small = four[:, :extra].reshape(devices_y, -1)[:, : 18 * shard].reshape(devices_y, 3, 6 * shard)
    small = gather_small(jnp.sum(small.astype(F32), axis=1).reshape(1, -1), "gx")
    small = small.reshape(devices_x, devices_y, 6, shard).transpose(2, 0, 1, 3).reshape(2, 3, width)

    two = lax.all_to_all(two, "gy", split_axis=0, concat_axis=0, tiled=True)
    live = (jnp.arange(img_count, dtype=jnp.int32) < image_counts[0]).astype(BF16)
    cot_own = cotangent * live[:, None, None]
    own = [
        jnp.concatenate([part[i : i + 1] for part in (media_features, latents, cot_own)], axis=1) for i in range(img_count)
    ]
    two, small, *own = tie(two, small, *own)
    ff_rows = two.reshape(devices_y * shard, 2 * ff_width)
    gains, biases = small[0], small[1]

    raw = {(0, i): own[i] for i in range(img_count)}
    if len(masks) == 4 and img_count == 2:
        slots = [(0, 0), (0, 1), (2, 0), (4, 0), (2, 1), (4, 1), (6, 0), (6, 1)]
        raw[2, 0], raw[4, 0], later = tie(swap(own[0], 2), swap(own[0], 4), own[1])
        raw[2, 0], raw[4, 0], ff_rows, mine = tie(raw[2, 0], raw[4, 0], ff_rows, mine)
        raw[2, 1], raw[4, 1], raw[6, 0] = swap(later, 2), swap(later, 4), swap(raw[2, 0], 4)
    else:
        slots = [(mask, i) for mask in masks for i in range(img_count)]
        for mask in masks[1:]:
            raw.update({(mask, i): swap(own[i], mask) for i in range(img_count)})
    ff_mine = lax.all_gather(ff_rows, "gx", axis=0, tiled=True)
    theirs = swap(mine, 1)

    steps, carried, out_parts = total // img_count, None, {}
    for step in range(steps):
        here = slots[step * img_count : (step + 1) * img_count]
        if carried:
            carried[0], *raws = tie(carried[0], *[raw[slot] for slot in here])
            raw.update(dict(zip(here, raws)))
        if (4, 1) in here and (6, 1) not in raw:
            raw[6, 1] = swap(raw[4, 1], 2)
        *carried, first_part, second_part = attend(
            pair, mine, theirs, small, [raw[slot] for slot in here], heads, patch, rows, step, total, carried
        )
        out_parts.update(dict(zip(here, (first_part, second_part))))
    joined_all, kv_all, qm_all = carried

    qm_all, *parts = tie(qm_all, *[raw[mask, i] for mask in masks for i in range(img_count)])
    cot_own_all = pick(parts, rows // lat, lat)
    out_parts = [
        swap(out_parts[mask, i], mask) if mask else out_parts[mask, i] for i in range(img_count) for mask in masks
    ]
    like_latents = lambda kind: (latents.shape, kind)
    attended, hidden_own = once(
        attended_kernel, [small, latents, *out_parts], [like_latents(F32), like_latents(BF16)]
    )
    hidden_own, cot_own_all = tie(hidden_own, cot_own_all)
    cot_other = swap(cot_own_all, 1)
    hidden = [part.reshape(img_count * lat, width) for part in spread(hidden_own).values()]
    hidden.append(swap(jnp.concatenate(hidden), 1))

    def plus(left, right):
        return (left.astype(F32) + right.astype(F32)).astype(BF16)

    def collect_pairs(parts):
        parts = [part.reshape(img_count, lat, width) for part in parts]
        return [parts[0]] + [swap(part, mask) for mask, part in zip(masks[1:], parts[1:])]

    total_of = lambda parts: sum(part.astype(F32) for part in parts)

    def summed(parts, other):
        return once(summed_kernel, [swap(other, 1), *parts], [(part.shape, BF16) for part in parts])

    hidden, cot_all, active, grad_upper, *hidden_parts, hidden_other = feed(hidden, cot_own_all, cot_other, ff_mine)
    ff_grads = feed_grads(hidden, cot_all, grad_upper, active)
    ff_grads, *hidden_parts = tie(ff_grads, *hidden_parts)
    hidden_parts = summed(hidden_parts, hidden_other)
    ff_part = lax.psum_scatter(ff_grads, "gx", scatter_dimension=0, tiled=True)
    hidden_parts = collect_pairs(hidden_parts)
    hidden_parts = [part.reshape(img_count * lat, width) for part in hidden_parts]
    grad_attended, grad_branch, sums_two = once(
        branch_kernel, [small, attended, cot_own, *hidden_parts],
        [like_latents(F32), like_latents(BF16), ((2, width), F32)],
    )
    branch = spread(grad_branch)
    ffn_parts = feed_out(active, ff_mine)
    *branch, ffn_part, ffn_other, ff_grads = tie(*branch.values(), *ffn_parts, ff_grads)
    branch = jnp.concatenate([branch[masks.index(mask)][i : i + 1] for mask, i in slots])

    arrays = pair, mine, theirs, branch, kv_all, qm_all, heads, patch
    back, carried, step = {}, None, steps - 1
    for count in (1, steps - 2, 1):
        *carried, results = attend_back(*arrays, step, count, img_count, carried)
        for index, part in enumerate(results):
            back[slots[(step - index // img_count) * img_count + index % img_count]] = part
        step -= count
    dkv_all, dquery_all = carried

    if (6, 0) in back:
        last = swap(back[6, 0], 4), swap(back[6, 1], 2)
        dkv_all, *last = tie(dkv_all, *last)
        through = once(
            through_kernel, [back[2, 0], last[0], back[4, 1], last[1]], [(back[2, 0].shape, BF16)] * 2
        )
    dkv_all, ff_part = tie(dkv_all, ff_part)
    keep, *give = attend_grads(
        pair, joined_all, branch.reshape(total * lat, width), dkv_all, dquery_all, qm_all, patch
    )
    if len(masks) == 4 and img_count == 2:
        keep, *direct = tie(keep, swap(back[4, 0], 4), swap(back[2, 1], 2), *through)
        through = direct[2:]
        arrived = [back[0, 0], swap(through[0], 2), direct[0], back[0, 1], direct[1], swap(through[1], 4)]
    else:
        arrived = [swap(back[mask, i], mask) if mask else back[mask, i] for i in range(img_count) for mask in masks]
    give = [swap(part, 1) for part in give]
    (at_grads,) = once(add_pieces_kernel, [keep, *give], [(keep.shape, BF16)])
    at_grads, ffn_other = tie(at_grads, ffn_other)
    shares = lax.psum_scatter(at_grads, "gx", scatter_dimension=0, tiled=True)
    ffn_part = ffn_part.reshape(len(masks), img_count * lat, width)
    ffn_parts = summed([ffn_part[i] for i in range(len(masks))], ffn_other)

    def home(part):
        return lax.all_to_all(part.reshape(devices_y, shard, -1), "gy", split_axis=0, concat_axis=0, tiled=True)

    each = len(arrived)
    *arrived, ff_part = tie(*arrived, *ffn_parts, ff_part)
    arrived, ffn_parts = arrived[:each], arrived[each:]
    grad_media, grad_latents, sums = once(
        rows_back_kernel, [small, sums_two, media_features, latents, grad_attended, *arrived],
        [(media_features.shape, F32), like_latents(F32), ((6, width), F32)],
    )
    sums = sum_small(sums)
    place = lax.axis_index("gx") * devices_y + lax.axis_index("gy")
    sums = lax.dynamic_slice_in_dim(sums, place * shard, shard, axis=1)

    shares, sums, ff_part, *ffn_parts = tie(shares, sums, home(ff_part), *collect_pairs(ffn_parts))
    grad_key, grad_value, grad_query, grad_out = ungroup(home(shares), 4, True)
    outputs = ((attended + total_of(ffn_parts)) * live.astype(F32)[:, None, None]).astype(BF16)
    grad_up, grad_down = ungroup(ff_part, 2, False)
    grad_down = grad_down.T
    return (
        outputs, grad_media, grad_latents, grad_query, grad_key, grad_value, grad_out.T, grad_up, grad_down,
        sums[:3], sums[3:],
    )


def solution(mesh):
    split = ("gx", "gy")
    images, first, second = P(split, None, None), P(split, None), P(None, split)
    return jax.shard_map(
        local,
        mesh=mesh,
        in_specs=(images, images, images, P(split), first, first, first, second, first, second, second, second),
        out_specs=(images, images, images, first, first, first, second, first, second, second, second),
        check_vma=False,
    )
```

```python
import functools
import math

import jax
import jax.numpy as jnp
from jax import lax
from jax.experimental import pallas as pl
from jax.experimental.pallas import tpu as pltpu
from jax.sharding import PartitionSpec as P

HEAD = 96
EPSILON = 1e-05
BF16 = jnp.bfloat16
F32 = jnp.float32
VMEM = 24 * 2**20
MOST = 56 * 2**20
SOME = pl.CostEstimate(flops=26 * 10**9, bytes_accessed=1024, transcendentals=0)
LITTLE = pl.CostEstimate(flops=1024, bytes_accessed=1024, transcendentals=0)


def product(left, right):
    return jnp.dot(left, right, preferred_element_type=F32)


def product_left(left, right):
    return lax.dot_general(left, right, (((0,), (0,)), ((), ())), preferred_element_type=F32)


def product_right(left, right):
    return lax.dot_general(left, right, (((1,), (1,)), ((), ())), preferred_element_type=F32)


def tie(*values):
    return lax.optimization_barrier(values)


def swap(block, mask, axis="gy"):
    count = lax.axis_size(axis)
    return lax.ppermute(block, axis, [(i, i ^ mask) for i in range(count)])


def far_masks():
    return [mask for mask in range(lax.axis_size("gy")) if mask % 2 == 0]


def spread(block):
    return {mask: swap(block, mask) if mask else block for mask in far_masks()}


def regroup_kernel(first_ref, *refs):
    *from_refs, to_ref = refs
    extra, half = first_ref.shape[0], len(from_refs) // 2
    groups = to_ref.shape[0] // 2
    cols = from_refs[0].shape[1] // groups
    for device in range(2 * groups):
        group, core = device // 2, device % 2
        to_ref[device, :extra] = first_ref[...]
        for index, from_ref in enumerate(from_refs[core * half : (core + 1) * half]):
            to_ref[device, extra:, index * cols : (index + 1) * cols] = from_ref[:, group * cols : (group + 1) * cols]


def regroup(first, devices, *weights):
    shard, width = weights[0].shape
    return pl.pallas_call(
        regroup_kernel,
        out_shape=jax.ShapeDtypeStruct((devices, first.shape[0] + shard, first.shape[1]), BF16),
        compiler_params=pltpu.CompilerParams(vmem_limit_bytes=VMEM),
        cost_estimate=LITTLE,
    )(first, *weights)


def ungroup_kernel(by_pair, from_ref, *to_refs):
    devices, _, width = from_ref.shape
    per = len(to_refs) // 2 if by_pair else len(to_refs)
    cols = width // per
    for index, to_ref in enumerate(to_refs):
        sources = range(index // per, devices, 2) if by_pair else range(devices)
        place = slice(index % per * cols, (index % per + 1) * cols)
        for position, device in enumerate(sources):
            to_ref[:, position * cols : (position + 1) * cols] = from_ref[device, :, place].astype(F32)


def ungroup(blocks, count, by_pair):
    devices, shard, width = blocks.shape
    return pl.pallas_call(
        functools.partial(ungroup_kernel, by_pair),
        out_shape=[jax.ShapeDtypeStruct((shard, devices * width // count), F32)] * count,
        compiler_params=pltpu.CompilerParams(vmem_limit_bytes=VMEM),
        cost_estimate=LITTLE,
    )(blocks)


def bits_of(count):
    bits, bit = [], 1
    while bit < count:
        bits.append(bit)
        bit *= 2
    return bits


def gather_small(rows, axis):
    place = lax.axis_index(axis)
    for bit in bits_of(lax.axis_size(axis)):
        other = swap(rows, bit, axis)
        upper = (place & bit) != 0
        rows = jnp.concatenate([jnp.where(upper, other, rows), jnp.where(upper, rows, other)])
    return rows


def normed(rows, gain, bias):
    average = jnp.mean(rows, axis=-1, keepdims=True)
    centred = rows - average
    spread_of = jnp.mean(centred * centred, axis=-1, keepdims=True)
    return centred * lax.rsqrt(spread_of + EPSILON) * gain + bias


def head_mask(rows, lanes, head):
    lane = lax.broadcasted_iota(jnp.int32, (rows, lanes), 1)
    return (lane >= head * HEAD) & (lane < (head + 1) * HEAD)


def stacked(rows, heads):
    count, lanes = rows.shape
    return jnp.concatenate(
        [jnp.where(head_mask(count, lanes, h), rows, jnp.zeros_like(rows)) for h in range(heads)]
    )


def unstacked(rows, heads):
    count, lanes = rows.shape[0] // heads, rows.shape[1]
    total = rows[:count]
    for h in range(1, heads):
        total = jnp.where(head_mask(count, lanes, h), rows[h * count : (h + 1) * count], total)
    return total


def softmax_rows(scores):
    top = jnp.max(scores, axis=-1, keepdims=True)
    raised = jnp.exp(scores - top)
    return raised / jnp.sum(raised, axis=-1, keepdims=True)


def load_weights(pair_ref, mine_ref, theirs_ref, kv_weights, qo_weights, sems):
    @pl.when(pair_ref[0] == 0)
    def _():
        pltpu.make_async_copy(theirs_ref, qo_weights, sems.at[1]).start()
        pltpu.make_async_copy(mine_ref, kv_weights, sems.at[0]).start()

    @pl.when(pair_ref[0] == 1)
    def _():
        pltpu.make_async_copy(mine_ref, qo_weights, sems.at[1]).start()
        pltpu.make_async_copy(theirs_ref, kv_weights, sems.at[0]).start()


def attend_kernel(heads, patch, scale, raws, given, pair_ref, mine_ref, theirs_ref, small_ref, *refs):
    *refs, kv_weights, qo_weights, sems = refs
    joined_ref, kv_ref, qm_ref, *out_refs = refs[raws + given :]
    count, rows, width = joined_ref.shape
    load_weights(pair_ref, mine_ref, theirs_ref, kv_weights, qo_weights, sems)
    for image, raw_ref in enumerate(refs[:raws]):
        media = normed(raw_ref[0, :patch].astype(F32), small_ref[0, 0:1], small_ref[1, 0:1])
        latent = normed(raw_ref[0, patch:rows].astype(F32), small_ref[0, 1:2], small_ref[1, 1:2])
        joined_ref[image, :patch] = media.astype(BF16)
        joined_ref[image, patch:] = latent.astype(BF16)
    pltpu.make_async_copy(mine_ref, kv_weights, sems.at[0]).wait()
    pltpu.make_async_copy(theirs_ref, qo_weights, sems.at[1]).wait()
    lat, cols = rows - patch, kv_weights.shape[1] // 2
    joined = joined_ref[...].reshape(count * rows, width)
    latent = joined_ref[:, patch:].reshape(count * lat, width)
    kv_ref[...] = product(joined, kv_weights[...]).astype(BF16).reshape(count, rows, 2 * cols)
    query = (product(latent, qo_weights[:, :cols]) * scale).astype(BF16)
    qm_ref[:, :, :cols] = query.reshape(count, lat, cols)
    mixed = []
    for image in range(count):
        probs = softmax_rows(product_right(stacked(query[image * lat : (image + 1) * lat], heads), kv_ref[image, :, :cols]))
        mixed.append(unstacked(product(probs.astype(BF16), kv_ref[image, :, cols:]), heads).astype(BF16))
    mixed = jnp.concatenate(mixed)
    qm_ref[:, :, cols:] = mixed.reshape(count, lat, cols)
    total = product_right(mixed, qo_weights[:, cols:]).astype(BF16).reshape(count, lat, width)
    for image, out_ref in enumerate(out_refs):
        out_ref[0] = total[image]


SMALL = pl.BlockSpec(memory_space=pltpu.SMEM)
ANY = pl.BlockSpec(memory_space=pl.ANY)


def weight_scratch(mine):
    return [pltpu.VMEM(mine.shape, BF16)] * 2 + [pltpu.SemaphoreType.DMA((2,))]


def attend(pair, mine, theirs, small, raws, heads, patch, rows, step, total, carried):
    width, cols = mine.shape
    lat, per = rows - patch, len(raws)
    part = lambda *shape: pl.BlockSpec((per,) + shape, lambda i: (step, 0, 0))
    given = list(carried or ())
    return pl.pallas_call(
        functools.partial(attend_kernel, heads, patch, HEAD ** (-0.5), per, len(given)),
        grid=(1,),
        in_specs=[SMALL, ANY, ANY, whole(small.shape)] + [whole(raw.shape) for raw in raws] + [ANY] * len(given),
        out_specs=[part(rows, width), part(rows, cols), part(lat, cols)] + [whole((1, lat, width))] * per,
        out_shape=[
            jax.ShapeDtypeStruct((total, rows, width), BF16),
            jax.ShapeDtypeStruct((total, rows, cols), BF16),
            jax.ShapeDtypeStruct((total, lat, cols), BF16),
        ]
        + [jax.ShapeDtypeStruct((1, lat, width), BF16)] * per,
        scratch_shapes=weight_scratch(mine),
        input_output_aliases={4 + per + i: i for i in range(len(given))},
        compiler_params=pltpu.CompilerParams(vmem_limit_bytes=VMEM),
        cost_estimate=LITTLE,
    )(pair, mine, theirs, small, *raws, *given)


def attend_back_kernel(heads, patch, scale, given, pair_ref, mine_ref, theirs_ref, branch_ref, kv_ref, qm_ref, *refs):
    *refs, kv_weights, qo_weights, sems = refs

    @pl.when(pl.program_id(0) == 0)
    def _():
        load_weights(pair_ref, mine_ref, theirs_ref, kv_weights, qo_weights, sems)
        pltpu.make_async_copy(theirs_ref, qo_weights, sems.at[1]).wait()

    dkv_ref, dquery_ref, *back_refs = refs[given:]
    count, lat, width = branch_ref.shape
    rows, cols = kv_ref.shape[1], kv_ref.shape[2] // 2
    branch = branch_ref[...].reshape(count * lat, width)
    all_mixed = product(branch, qo_weights[:, cols:]).astype(BF16)
    for image in range(count):
        keys, values = kv_ref[image, :, :cols], kv_ref[image, :, cols:]
        query = stacked(qm_ref[image, :, :cols], heads)
        probs = softmax_rows(product_right(query, keys))
        grad_mixed = stacked(all_mixed[image * lat : (image + 1) * lat], heads)
        grad_probs = product_right(grad_mixed, values)
        inner = jnp.sum(grad_probs * probs, axis=-1, keepdims=True)
        grad_scores = (probs * (grad_probs - inner)).astype(BF16)
        dquery_ref[image] = unstacked(product(grad_scores, keys), heads).astype(BF16)
        dkv_ref[image, :, :cols] = product_left(grad_scores, query).astype(BF16)
        dkv_ref[image, :, cols:] = product_left(probs.astype(BF16), grad_mixed).astype(BF16)

    @pl.when(pl.program_id(0) == 0)
    def _():
        pltpu.make_async_copy(mine_ref, kv_weights, sems.at[0]).wait()

    back = product_right(dkv_ref[...].reshape(count * rows, 2 * cols), kv_weights[...]).reshape(count, rows, width)
    extra = product_right(dquery_ref[...].reshape(count * lat, cols), qo_weights[:, :cols]) * scale
    extra = extra.reshape(count, lat, width)
    for index, back_ref in enumerate(back_refs):

        @pl.when(pl.program_id(0) == index // count)
        def _(back_ref=back_ref, image=index % count):
            back_ref[0, :patch] = back[image, :patch].astype(BF16)
            back_ref[0, patch:] = (back[image, patch:] + extra[image]).astype(BF16)


def attend_back(pair, mine, theirs, branch, kv, qm, heads, patch, first, steps, per, carried):
    total, rows, cols = kv.shape
    lat, width = branch.shape[1:]
    part = lambda *shape: pl.BlockSpec((per,) + shape, lambda i: (first - i, 0, 0))
    given = list(carried or ())
    dkv, dquery, *backs = pl.pallas_call(
        functools.partial(attend_back_kernel, heads, patch, HEAD ** (-0.5), len(given)),
        grid=(steps,),
        in_specs=[SMALL, ANY, ANY, part(lat, width), part(rows, cols), part(lat, cols)] + [ANY] * len(given),
        out_specs=[part(rows, cols), part(lat, cols // 2)] + [whole((1, rows, width))] * (steps * per),
        out_shape=[
            jax.ShapeDtypeStruct((total, rows, cols), BF16),
            jax.ShapeDtypeStruct((total, lat, cols // 2), BF16),
        ]
        + [jax.ShapeDtypeStruct((1, rows, width), BF16)] * (steps * per),
        scratch_shapes=weight_scratch(mine),
        input_output_aliases={6 + i: i for i in range(len(given))},
        compiler_params=pltpu.CompilerParams(vmem_limit_bytes=VMEM),
        cost_estimate=SOME,
    )(pair, mine, theirs, branch, kv, qm, *given)
    return dkv, dquery, backs


def feed_kernel(tile, parts, cot_ref, cot_other_ref, weights_ref, *refs):
    hidden_refs, refs = refs[:parts], refs[parts:]
    all_ref, cots_ref, active_ref, upper_ref, *part_refs, weights, total_ref, sem = refs
    cols = weights_ref.shape[1] // 2
    copy = pltpu.make_async_copy(weights_ref, weights, sem)
    copy.start()
    start = 0
    for hidden_ref in hidden_refs:
        all_ref[start : start + hidden_ref.shape[0]] = hidden_ref[...]
        start += hidden_ref.shape[0]
    cots_ref[: start // 2] = cot_ref[...]
    cots_ref[start // 2 :] = cot_other_ref[...]
    rows = all_ref.shape[0]
    block = math.gcd(rows, 256)
    copy.wait()
    for index in range(cols // tile):
        place = slice(index * tile, (index + 1) * tile)
        up, down = weights[:, place], weights[:, cols + index * tile : cols + (index + 1) * tile]
        for first in range(0, rows, block):
            here = slice(first, first + block)
            upper = product(all_ref[here], up)
            cdf = 0.5 * (1.0 + lax.erf(upper * (0.5**0.5)))
            slope = cdf + upper * jnp.exp(-0.5 * upper * upper) * (0.5 / math.pi) ** 0.5
            grad_upper = (slope * product(cots_ref[here], down)).astype(BF16)
            active_ref[here, place] = (upper * cdf).astype(BF16)
            upper_ref[here, place] = grad_upper
    for first in range(0, rows, block):
        here = slice(first, first + block)
        total_ref[here] = product_right(upper_ref[here], weights[:, :cols])
    start = 0
    for part_ref in part_refs:
        part_ref[...] = total_ref[start : start + part_ref.shape[0]].astype(BF16)
        start += part_ref.shape[0]


def feed(hidden, cot, cot_other, weights):
    width = cot.shape[1]
    rows = 2 * cot.shape[0]
    cols = weights.shape[1] // 2
    tile = 256 if cols % 256 == 0 else math.gcd(cols, 384)
    shapes = [(rows, width)] * 2 + [(rows, cols)] * 2 + [part.shape for part in hidden]
    return pl.pallas_call(
        functools.partial(feed_kernel, tile, len(hidden)),
        grid=(1,),
        in_specs=[whole(cot.shape)] * 2 + [ANY] + [whole(part.shape) for part in hidden],
        out_specs=[whole(shape) for shape in shapes],
        out_shape=[jax.ShapeDtypeStruct(shape, BF16) for shape in shapes],
        scratch_shapes=[pltpu.VMEM(weights.shape, BF16), pltpu.VMEM((rows, width), F32), pltpu.SemaphoreType.DMA],
        compiler_params=pltpu.CompilerParams(vmem_limit_bytes=MOST),
        cost_estimate=LITTLE,
    )(cot, cot_other, weights, *hidden)


def feed_out_kernel(active_ref, weights_ref, own_ref, other_ref):
    rows = own_ref.shape[0]
    own_ref[...] = product_right(active_ref[:rows], weights_ref[...]).astype(BF16)
    other_ref[...] = product_right(active_ref[rows:], weights_ref[...]).astype(BF16)


def feed_out(active, weights):
    rows, cols = active.shape
    width = weights.shape[0]
    return pl.pallas_call(
        feed_out_kernel,
        grid=(1,),
        in_specs=[whole(active.shape), pl.BlockSpec((width, cols), lambda i: (0, 1))],
        out_specs=[whole((rows // 2, width))] * 2,
        out_shape=[jax.ShapeDtypeStruct((rows // 2, width), BF16)] * 2,
        compiler_params=pltpu.CompilerParams(vmem_limit_bytes=VMEM),
        cost_estimate=LITTLE,
    )(active, weights)


def feed_grads_kernel(hidden_ref, cot_ref, upper_ref, active_ref, to_ref):
    half = upper_ref.shape[1]
    to_ref[:, :half] = product_left(hidden_ref[...], upper_ref[...]).astype(BF16)
    to_ref[:, half:] = product_left(cot_ref[...], active_ref[...]).astype(BF16)


def row_tiles(width):
    return width // math.gcd(width, 384)


def feed_grads(hidden, cot, upper, active):
    rows, width = hidden.shape
    cols = upper.shape[1]
    steps = row_tiles(width)
    left = pl.BlockSpec((rows, width // steps), lambda i: (0, i))
    right = pl.BlockSpec((rows, cols), lambda i: (0, 0))
    return pl.pallas_call(
        feed_grads_kernel,
        grid=(steps,),
        in_specs=[left, left, right, right],
        out_specs=pl.BlockSpec((width // steps, 2 * cols), lambda i: (i, 0)),
        out_shape=jax.ShapeDtypeStruct((width, 2 * cols), BF16),
        compiler_params=pltpu.CompilerParams(vmem_limit_bytes=VMEM),
        cost_estimate=LITTLE,
    )(hidden, cot, upper, active)


def add_pieces_kernel(first_ref, *refs):
    *piece_refs, to_ref = refs
    rows = piece_refs[0].shape[0]
    for index, piece_ref in enumerate(piece_refs):
        place = slice(index * rows, (index + 1) * rows)
        to_ref[place] = (first_ref[place].astype(F32) + piece_ref[...].astype(F32)).astype(BF16)


def pick_kernel(*refs):
    *from_refs, to_ref = refs
    rows = from_refs[0].shape[1]
    for index, from_ref in enumerate(from_refs):
        to_ref[index * rows : (index + 1) * rows] = from_ref[0]


def pick(parts, block, rows):
    width = parts[0].shape[2]
    return pl.pallas_call(
        pick_kernel,
        grid=(1,),
        in_specs=[pl.BlockSpec((1, rows, width), lambda i: (0, block, 0))] * len(parts),
        out_specs=pl.BlockSpec((len(parts) * rows, width), lambda i: (0, 0)),
        out_shape=jax.ShapeDtypeStruct((len(parts) * rows, width), BF16),
        compiler_params=pltpu.CompilerParams(vmem_limit_bytes=VMEM),
        cost_estimate=LITTLE,
    )(*parts)


def attend_grads_kernel(patch, scale, pair_ref, joined_ref, branch_ref, dkv_ref, dquery_ref, qm_ref, keep_ref, *give_refs):
    count, rows, tile = joined_ref.shape
    lat, cols = rows - patch, dquery_ref.shape[2]
    joined = joined_ref[...].reshape(count * rows, tile)
    latent = joined_ref[:, patch:].reshape(count * lat, tile)
    kv = product_left(joined, dkv_ref[...].reshape(count * rows, 2 * cols)).astype(BF16)
    query = (product_left(latent, dquery_ref[...].reshape(count * lat, cols)) * scale).astype(BF16)
    out = product_left(branch_ref[...], qm_ref[:, :, cols:].reshape(count * lat, cols)).astype(BF16)

    @pl.when(pair_ref[0] == 0)
    def _():
        keep_ref[...] = kv

    @pl.when(pair_ref[0] == 1)
    def _():
        keep_ref[:, :cols] = query
        keep_ref[:, cols:] = out

    for step, give_ref in enumerate(give_refs):

        @pl.when((pl.program_id(0) == step) & (pair_ref[0] == 0))
        def _(give_ref=give_ref):
            give_ref[:, :cols] = query
            give_ref[:, cols:] = out

        @pl.when((pl.program_id(0) == step) & (pair_ref[0] == 1))
        def _(give_ref=give_ref):
            give_ref[...] = kv


def attend_grads(pair, joined, branch, dkv, dquery, qm, patch):
    total, rows, width = joined.shape
    lat, cols = rows - patch, dkv.shape[2]
    steps = row_tiles(width)
    tile = pl.BlockSpec((width // steps, cols), lambda i: (i, 0))
    return pl.pallas_call(
        functools.partial(attend_grads_kernel, patch, HEAD ** (-0.5)),
        grid=(steps,),
        in_specs=[
            SMALL,
            pl.BlockSpec((total, rows, width // steps), lambda i: (0, 0, i)),
            pl.BlockSpec((total * lat, width // steps), lambda i: (0, i)),
            whole(dkv.shape), whole(dquery.shape), whole(qm.shape),
        ],
        out_specs=[tile] + [whole((width // steps, cols))] * steps,
        out_shape=[jax.ShapeDtypeStruct((width, cols), BF16)] + [jax.ShapeDtypeStruct((width // steps, cols), BF16)] * steps,
        compiler_params=pltpu.CompilerParams(vmem_limit_bytes=VMEM),
        cost_estimate=LITTLE,
    )(pair, joined, branch, dkv, dquery, qm)


def whole(shape):
    return pl.BlockSpec(shape, lambda *_: (0,) * len(shape))


def once(kernel, operands, shapes, cost=LITTLE):
    return pl.pallas_call(
        kernel,
        grid=(1,),
        in_specs=[whole(operand.shape) for operand in operands],
        out_specs=[whole(shape) for shape, _ in shapes],
        out_shape=[jax.ShapeDtypeStruct(shape, kind) for shape, kind in shapes],
        compiler_params=pltpu.CompilerParams(vmem_limit_bytes=VMEM),
        cost_estimate=cost,
    )(*operands)


def attended_kernel(small_ref, latent_ref, *refs):
    *part_refs, attended_ref, hidden_ref = refs
    images = latent_ref.shape[0]
    each = len(part_refs) // images
    for image in range(images):
        total = latent_ref[image].astype(F32)
        for part_ref in part_refs[image * each : (image + 1) * each]:
            total = total + part_ref[0].astype(F32)
        attended_ref[image] = total
        hidden_ref[image] = normed(total, small_ref[0, 2:3], small_ref[1, 2:3]).astype(BF16)


def summed_kernel(other_ref, *refs):
    count = len(refs) // 2
    rows = other_ref.shape[0] // count
    for index in range(count):
        other = other_ref[index * rows : (index + 1) * rows].astype(F32)
        refs[count + index][...] = (refs[index][...].astype(F32) + other).astype(BF16)


def through_kernel(*refs):
    for index in range(2):
        left_ref, right_ref, to_ref = refs[2 * index], refs[2 * index + 1], refs[4 + index]
        to_ref[...] = (left_ref[...].astype(F32) + right_ref[...].astype(F32)).astype(BF16)


def norm_back(rows, gain, grad):
    average = jnp.mean(rows, axis=-1, keepdims=True)
    centred = rows - average
    inverse = lax.rsqrt(jnp.mean(centred * centred, axis=-1, keepdims=True) + EPSILON)
    unit = centred * inverse
    scaled = grad * gain
    first = jnp.mean(scaled, axis=-1, keepdims=True)
    second = jnp.mean(scaled * unit, axis=-1, keepdims=True)
    back = inverse * (scaled - first - unit * second)
    return back, jnp.sum(grad * unit, axis=0, keepdims=True), jnp.sum(grad, axis=0, keepdims=True)


def branch_kernel(small_ref, attended_ref, cot_ref, *refs):
    *part_refs, grad_ref, branch_ref, sums_ref = refs
    images, lat, width = attended_ref.shape
    grad = sum(part_ref[...].astype(F32) for part_ref in part_refs)
    back, gain, bias = norm_back(attended_ref[...].reshape(images * lat, width), small_ref[0, 2:3], grad)
    total = (cot_ref[...].reshape(images * lat, width).astype(F32) + back).reshape(images, lat, width)
    grad_ref[...] = total
    branch_ref[...] = total.astype(BF16)
    sums_ref[0:1] = gain
    sums_ref[1:2] = bias


def rows_back_kernel(small_ref, sums_two_ref, media_ref, latent_ref, grad_ref, *refs):
    *part_refs, media_to_ref, latent_to_ref, sums_ref = refs
    images, patch, _ = media_ref.shape
    each = len(part_refs) // images
    totals = None
    for image in range(images):
        parts = part_refs[image * each : (image + 1) * each]
        grad = sum(part_ref[0, :patch].astype(F32) for part_ref in parts)
        media, gain_zero, bias_zero = norm_back(media_ref[image].astype(F32), small_ref[0, 0:1], grad)
        media_to_ref[image] = media
        grad = sum(part_ref[0, patch:].astype(F32) for part_ref in parts)
        latent, gain_one, bias_one = norm_back(latent_ref[image].astype(F32), small_ref[0, 1:2], grad)
        latent_to_ref[image] = grad_ref[image] + latent
        terms = gain_zero, gain_one, bias_zero, bias_one
        totals = terms if totals is None else [left + right for left, right in zip(totals, terms)]
    for row, total in zip((0, 1, 3, 4), totals):
        sums_ref[row : row + 1] = total
    sums_ref[2:3] = sums_two_ref[0:1]
    sums_ref[5:6] = sums_two_ref[1:2]


def in_thirds(values):
    parts, rest = [], values
    for _ in range(3):
        part = lax.reduce_precision(rest, exponent_bits=8, mantissa_bits=7)
        parts.append(part.astype(BF16))
        rest = rest - part
    return jnp.stack(parts)


def local(media_features, latents, cotangent, image_counts, w_query, w_key, w_value, w_out, w_up, w_down,
          norm_gains, norm_biases):
    devices_x, devices_y = lax.axis_size("gx"), lax.axis_size("gy")
    masks = far_masks()
    img_count, lat, width = latents.shape
    patch = media_features.shape[1]
    rows = patch + lat
    shard = w_query.shape[0]
    head_width = width // devices_y
    heads = 2 * head_width // HEAD
    pair = (lax.axis_index("gy") % 2).astype(jnp.int32).reshape(1)
    ff_width = w_up.shape[1] // devices_y
    total = img_count * len(masks)

    four_width = 4 * head_width
    small = in_thirds(jnp.stack([norm_gains, norm_biases])).reshape(-1)
    extra = -(-small.size // (16 * four_width)) * 16
    small = jnp.pad(small, (0, extra * four_width - small.size)).reshape(extra, four_width)
    four = regroup(small, devices_y, w_key, w_value, w_query, w_out.T)
    four = lax.all_to_all(four, "gy", split_axis=0, concat_axis=0, tiled=True)
    mine = lax.all_gather(four[:, extra:].reshape(devices_y * shard, four_width), "gx", axis=0, tiled=True)

    two = jnp.concatenate(
        [part.reshape(shard, devices_y, ff_width).transpose(1, 0, 2) for part in (w_up, w_down.T)], axis=2
    )
    two, four = tie(two, four)
    small = four[:, :extra].reshape(devices_y, -1)[:, : 18 * shard].reshape(devices_y, 3, 6 * shard)
    small = gather_small(jnp.sum(small.astype(F32), axis=1).reshape(1, -1), "gx")
    small = small.reshape(devices_x, devices_y, 6, shard).transpose(2, 0, 1, 3).reshape(2, 3, width)

    two = lax.all_to_all(two, "gy", split_axis=0, concat_axis=0, tiled=True)
    live = (jnp.arange(img_count, dtype=jnp.int32) < image_counts[0]).astype(BF16)
    cot_own = cotangent * live[:, None, None]
    own = [
        jnp.concatenate([part[i : i + 1] for part in (media_features, latents, cot_own)], axis=1) for i in range(img_count)
    ]
    two, small, *own = tie(two, small, *own)
    ff_rows = two.reshape(devices_y * shard, 2 * ff_width)
    gains, biases = small[0], small[1]

    raw = {(0, i): own[i] for i in range(img_count)}
    if len(masks) == 4 and img_count == 2:
        slots = [(0, 0), (0, 1), (2, 0), (4, 0), (2, 1), (4, 1), (6, 0), (6, 1)]
        raw[2, 0], raw[4, 0], later = tie(swap(own[0], 2), swap(own[0], 4), own[1])
        raw[2, 0], raw[4, 0], ff_rows, mine = tie(raw[2, 0], raw[4, 0], ff_rows, mine)
        raw[2, 1], raw[4, 1], raw[6, 0] = swap(later, 2), swap(later, 4), swap(raw[2, 0], 4)
    else:
        slots = [(mask, i) for mask in masks for i in range(img_count)]
        for mask in masks[1:]:
            raw.update({(mask, i): swap(own[i], mask) for i in range(img_count)})
    ff_mine = lax.all_gather(ff_rows, "gx", axis=0, tiled=True)
    theirs = swap(mine, 1)

    steps, carried, out_parts = total // img_count, None, {}
    for step in range(steps):
        here = slots[step * img_count : (step + 1) * img_count]
        if carried:
            carried[0], *raws = tie(carried[0], *[raw[slot] for slot in here])
            raw.update(dict(zip(here, raws)))
        if (4, 1) in here and (6, 1) not in raw:
            raw[6, 1] = swap(raw[4, 1], 2)
        *carried, first_part, second_part = attend(
            pair, mine, theirs, small, [raw[slot] for slot in here], heads, patch, rows, step, total, carried
        )
        out_parts.update(dict(zip(here, (first_part, second_part))))
    joined_all, kv_all, qm_all = carried

    qm_all, *parts = tie(qm_all, *[raw[mask, i] for mask in masks for i in range(img_count)])
    cot_own_all = pick(parts, rows // lat, lat)
    out_parts = [
        swap(out_parts[mask, i], mask) if mask else out_parts[mask, i] for i in range(img_count) for mask in masks
    ]
    like_latents = lambda kind: (latents.shape, kind)
    attended, hidden_own = once(
        attended_kernel, [small, latents, *out_parts], [like_latents(F32), like_latents(BF16)]
    )
    hidden_own, cot_own_all = tie(hidden_own, cot_own_all)
    cot_other = swap(cot_own_all, 1)
    hidden = [part.reshape(img_count * lat, width) for part in spread(hidden_own).values()]
    hidden.append(swap(jnp.concatenate(hidden), 1))

    def plus(left, right):
        return (left.astype(F32) + right.astype(F32)).astype(BF16)

    def collect_pairs(parts):
        parts = [part.reshape(img_count, lat, width) for part in parts]
        return [parts[0]] + [swap(part, mask) for mask, part in zip(masks[1:], parts[1:])]

    total_of = lambda parts: sum(part.astype(F32) for part in parts)

    def summed(parts, other):
        return once(summed_kernel, [swap(other, 1), *parts], [(part.shape, BF16) for part in parts])

    hidden, cot_all, active, grad_upper, *hidden_parts, hidden_other = feed(hidden, cot_own_all, cot_other, ff_mine)
    hidden_parts = summed(hidden_parts, hidden_other)
    grad_upper, *hidden_parts = tie(grad_upper, *hidden_parts)
    ff_grads = feed_grads(hidden, cot_all, grad_upper, active)
    ff_part = lax.psum_scatter(ff_grads, "gx", scatter_dimension=0, tiled=True)
    hidden_parts = collect_pairs(hidden_parts)
    hidden_parts = [part.reshape(img_count * lat, width) for part in hidden_parts]
    grad_attended, grad_branch, sums_two = once(
        branch_kernel, [small, attended, cot_own, *hidden_parts],
        [like_latents(F32), like_latents(BF16), ((2, width), F32)],
    )
    branch = spread(grad_branch)
    ffn_parts = feed_out(active, ff_mine)
    *branch, ffn_part, ffn_other = tie(*branch.values(), *ffn_parts)
    branch = jnp.concatenate([branch[masks.index(mask)][i : i + 1] for mask, i in slots])

    arrays = pair, mine, theirs, branch, kv_all, qm_all, heads, patch
    back, carried, step = {}, None, steps - 1
    for count in (1, steps - 1):
        *carried, results = attend_back(*arrays, step, count, img_count, carried)
        for index, part in enumerate(results):
            back[slots[(step - index // img_count) * img_count + index % img_count]] = part
        step -= count
    dkv_all, dquery_all = carried

    if len(masks) == 4 and img_count == 2:
        last = swap(back[6, 0], 4), swap(back[6, 1], 2)
        through = once(
            through_kernel, [back[2, 0], last[0], back[4, 1], last[1]], [(back[2, 0].shape, BF16)] * 2
        )
        dkv_all, *through = tie(dkv_all, *through)
    def home(part):
        return lax.all_to_all(part.reshape(devices_y, shard, -1), "gy", split_axis=0, concat_axis=0, tiled=True)

    keep, *give = attend_grads(
        pair, joined_all, branch.reshape(total * lat, width), dkv_all, dquery_all, qm_all, patch
    )
    if len(masks) == 4 and img_count == 2:
        keep, ff_part, *through = tie(keep, ff_part, swap(through[0], 2), swap(through[1], 4), back[4, 0], back[2, 1])
        direct = swap(through[2], 4), swap(through[3], 2)
        arrived = [back[0, 0], through[0], direct[0], back[0, 1], direct[1], through[1]]
    else:
        arrived = [swap(back[mask, i], mask) if mask else back[mask, i] for i in range(img_count) for mask in masks]
    give = [swap(part, 1) for part in give]
    (at_grads,) = once(add_pieces_kernel, [keep, *give], [(keep.shape, BF16)])
    at_grads, ffn_other = tie(at_grads, ffn_other)
    shares = lax.psum_scatter(at_grads, "gx", scatter_dimension=0, tiled=True)
    ffn_part = ffn_part.reshape(len(masks), img_count * lat, width)
    ffn_parts = summed([ffn_part[i] for i in range(len(masks))], ffn_other)

    each = len(arrived)
    *arrived, ff_part = tie(*arrived, *ffn_parts, ff_part)
    arrived, ffn_parts = arrived[:each], arrived[each:]
    grad_media, grad_latents, sums = once(
        rows_back_kernel, [small, sums_two, media_features, latents, grad_attended, *arrived],
        [(media_features.shape, F32), like_latents(F32), ((6, width), F32)],
        cost=SOME,
    )
    *ffn_parts, sums = tie(*collect_pairs(ffn_parts), sums + swap(sums, 1))
    sums = sum([sums] + [swap(sums, mask) for mask in masks[1:]])
    sums = sum([sums] + [swap(sums, mask, "gx") for mask in range(1, devices_x)])
    place = lax.axis_index("gx") * devices_y + lax.axis_index("gy")
    sums = lax.dynamic_slice_in_dim(sums, place * shard, shard, axis=1)

    shares, sums, ff_part, *ffn_parts = tie(shares, sums, home(ff_part), *ffn_parts)
    grad_key, grad_value, grad_query, grad_out = ungroup(home(shares), 4, True)
    outputs = ((attended + total_of(ffn_parts)) * live.astype(F32)[:, None, None]).astype(BF16)
    grad_up, grad_down = ungroup(ff_part, 2, False)
    grad_down = grad_down.T
    return (
        outputs, grad_media, grad_latents, grad_query, grad_key, grad_value, grad_out.T, grad_up, grad_down,
        sums[:3], sums[3:],
    )


def solution(mesh):
    split = ("gx", "gy")
    images, first, second = P(split, None, None), P(split, None), P(None, split)
    return jax.shard_map(
        local,
        mesh=mesh,
        in_specs=(images, images, images, P(split), first, first, first, second, first, second, second, second),
        out_specs=(images, images, images, first, first, first, second, first, second, second, second),
        check_vma=False,
    )
```

```python
import functools
import math

import jax
import jax.numpy as jnp
from jax import lax
from jax.experimental import pallas as pl
from jax.experimental.pallas import tpu as pltpu
from jax.sharding import PartitionSpec as P

HEAD = 96
EPSILON = 1e-05
BF16 = jnp.bfloat16
F32 = jnp.float32
VMEM = 24 * 2**20
MOST = 56 * 2**20
SOME = pl.CostEstimate(flops=26 * 10**9, bytes_accessed=1024, transcendentals=0)
LITTLE = pl.CostEstimate(flops=1024, bytes_accessed=1024, transcendentals=0)


def product(left, right):
    return jnp.dot(left, right, preferred_element_type=F32)


def product_left(left, right):
    return lax.dot_general(left, right, (((0,), (0,)), ((), ())), preferred_element_type=F32)


def product_right(left, right):
    return lax.dot_general(left, right, (((1,), (1,)), ((), ())), preferred_element_type=F32)


def tie(*values):
    return lax.optimization_barrier(values)


def swap(block, mask, axis="gy"):
    count = lax.axis_size(axis)
    return lax.ppermute(block, axis, [(i, i ^ mask) for i in range(count)])


def far_masks():
    return [mask for mask in range(lax.axis_size("gy")) if mask % 2 == 0]


def spread(block):
    return {mask: swap(block, mask) if mask else block for mask in far_masks()}


def regroup_kernel(first_ref, *refs):
    *from_refs, to_ref = refs
    extra, half = first_ref.shape[0], len(from_refs) // 2
    groups = to_ref.shape[0] // 2
    cols = from_refs[0].shape[1] // groups
    for device in range(2 * groups):
        group, core = device // 2, device % 2
        to_ref[device, :extra] = first_ref[...]
        for index, from_ref in enumerate(from_refs[core * half : (core + 1) * half]):
            to_ref[device, extra:, index * cols : (index + 1) * cols] = from_ref[:, group * cols : (group + 1) * cols]


def regroup(first, devices, *weights):
    shard, width = weights[0].shape
    return pl.pallas_call(
        regroup_kernel,
        out_shape=jax.ShapeDtypeStruct((devices, first.shape[0] + shard, first.shape[1]), BF16),
        compiler_params=pltpu.CompilerParams(vmem_limit_bytes=MOST),
        cost_estimate=LITTLE,
    )(first, *weights)


def ungroup_kernel(by_pair, from_ref, *to_refs):
    devices, _, width = from_ref.shape
    per = len(to_refs) // 2 if by_pair else len(to_refs)
    cols = width // per
    for index, to_ref in enumerate(to_refs):
        sources = range(index // per, devices, 2) if by_pair else range(devices)
        place = slice(index % per * cols, (index % per + 1) * cols)
        for position, device in enumerate(sources):
            to_ref[:, position * cols : (position + 1) * cols] = from_ref[device, :, place].astype(F32)


def ungroup(blocks, count, by_pair):
    devices, shard, width = blocks.shape
    return pl.pallas_call(
        functools.partial(ungroup_kernel, by_pair),
        out_shape=[jax.ShapeDtypeStruct((shard, devices * width // count), F32)] * count,
        compiler_params=pltpu.CompilerParams(vmem_limit_bytes=VMEM),
        cost_estimate=LITTLE,
    )(blocks)


def bits_of(count):
    bits, bit = [], 1
    while bit < count:
        bits.append(bit)
        bit *= 2
    return bits


def gather_small(rows, axis):
    place = lax.axis_index(axis)
    for bit in bits_of(lax.axis_size(axis)):
        other = swap(rows, bit, axis)
        upper = (place & bit) != 0
        rows = jnp.concatenate([jnp.where(upper, other, rows), jnp.where(upper, rows, other)])
    return rows


def normed(rows, gain, bias):
    average = jnp.mean(rows, axis=-1, keepdims=True)
    centred = rows - average
    spread_of = jnp.mean(centred * centred, axis=-1, keepdims=True)
    return centred * lax.rsqrt(spread_of + EPSILON) * gain + bias


def head_mask(rows, lanes, head):
    lane = lax.broadcasted_iota(jnp.int32, (rows, lanes), 1)
    return (lane >= head * HEAD) & (lane < (head + 1) * HEAD)


def stacked(rows, heads):
    count, lanes = rows.shape
    return jnp.concatenate(
        [jnp.where(head_mask(count, lanes, h), rows, jnp.zeros_like(rows)) for h in range(heads)]
    )


def unstacked(rows, heads):
    count, lanes = rows.shape[0] // heads, rows.shape[1]
    total = rows[:count]
    for h in range(1, heads):
        total = jnp.where(head_mask(count, lanes, h), rows[h * count : (h + 1) * count], total)
    return total


def softmax_rows(scores):
    top = jnp.max(scores, axis=-1, keepdims=True)
    raised = jnp.exp(scores - top)
    return raised / jnp.sum(raised, axis=-1, keepdims=True)


def load_weights(pair_ref, mine_ref, theirs_ref, kv_weights, qo_weights, sems):
    @pl.when(pair_ref[0] == 0)
    def _():
        pltpu.make_async_copy(theirs_ref, qo_weights, sems.at[1]).start()
        pltpu.make_async_copy(mine_ref, kv_weights, sems.at[0]).start()

    @pl.when(pair_ref[0] == 1)
    def _():
        pltpu.make_async_copy(mine_ref, qo_weights, sems.at[1]).start()
        pltpu.make_async_copy(theirs_ref, kv_weights, sems.at[0]).start()


def attend_kernel(heads, patch, scale, raws, given, pair_ref, mine_ref, theirs_ref, small_ref, *refs):
    *refs, kv_weights, qo_weights, sems = refs
    joined_ref, kv_ref, qm_ref, *out_refs = refs[raws + given :]
    count, rows, width = joined_ref.shape
    load_weights(pair_ref, mine_ref, theirs_ref, kv_weights, qo_weights, sems)
    for image, raw_ref in enumerate(refs[:raws]):
        media = normed(raw_ref[0, :patch].astype(F32), small_ref[0, 0:1], small_ref[1, 0:1])
        latent = normed(raw_ref[0, patch:rows].astype(F32), small_ref[0, 1:2], small_ref[1, 1:2])
        joined_ref[image, :patch] = media.astype(BF16)
        joined_ref[image, patch:] = latent.astype(BF16)
    pltpu.make_async_copy(mine_ref, kv_weights, sems.at[0]).wait()
    pltpu.make_async_copy(theirs_ref, qo_weights, sems.at[1]).wait()
    lat, cols = rows - patch, kv_weights.shape[1] // 2
    joined = joined_ref[...].reshape(count * rows, width)
    latent = joined_ref[:, patch:].reshape(count * lat, width)
    kv_ref[...] = product(joined, kv_weights[...]).astype(BF16).reshape(count, rows, 2 * cols)
    query = (product(latent, qo_weights[:, :cols]) * scale).astype(BF16)
    qm_ref[:, :, :cols] = query.reshape(count, lat, cols)
    mixed = []
    for image in range(count):
        probs = softmax_rows(product_right(stacked(query[image * lat : (image + 1) * lat], heads), kv_ref[image, :, :cols]))
        mixed.append(unstacked(product(probs.astype(BF16), kv_ref[image, :, cols:]), heads).astype(BF16))
    mixed = jnp.concatenate(mixed)
    qm_ref[:, :, cols:] = mixed.reshape(count, lat, cols)
    total = product_right(mixed, qo_weights[:, cols:]).astype(BF16).reshape(count, lat, width)
    for image, out_ref in enumerate(out_refs):
        out_ref[0] = total[image]


SMALL = pl.BlockSpec(memory_space=pltpu.SMEM)
ANY = pl.BlockSpec(memory_space=pl.ANY)


def weight_scratch(mine):
    return [pltpu.VMEM(mine.shape, BF16)] * 2 + [pltpu.SemaphoreType.DMA((2,))]


def attend(pair, mine, theirs, small, raws, heads, patch, rows, step, total, carried):
    width, cols = mine.shape
    lat, per = rows - patch, len(raws)
    part = lambda *shape: pl.BlockSpec((per,) + shape, lambda i: (step, 0, 0))
    given = list(carried or ())
    return pl.pallas_call(
        functools.partial(attend_kernel, heads, patch, HEAD ** (-0.5), per, len(given)),
        grid=(1,),
        in_specs=[SMALL, ANY, ANY, whole(small.shape)] + [whole(raw.shape) for raw in raws] + [ANY] * len(given),
        out_specs=[part(rows, width), part(rows, cols), part(lat, cols)] + [whole((1, lat, width))] * per,
        out_shape=[
            jax.ShapeDtypeStruct((total, rows, width), BF16),
            jax.ShapeDtypeStruct((total, rows, cols), BF16),
            jax.ShapeDtypeStruct((total, lat, cols), BF16),
        ]
        + [jax.ShapeDtypeStruct((1, lat, width), BF16)] * per,
        scratch_shapes=weight_scratch(mine),
        input_output_aliases={4 + per + i: i for i in range(len(given))},
        compiler_params=pltpu.CompilerParams(vmem_limit_bytes=VMEM),
        cost_estimate=LITTLE,
    )(pair, mine, theirs, small, *raws, *given)


def attend_back_kernel(heads, patch, scale, given, pair_ref, mine_ref, theirs_ref, branch_ref, kv_ref, qm_ref, *refs):
    *refs, kv_weights, qo_weights, sems = refs

    @pl.when(pl.program_id(0) == 0)
    def _():
        load_weights(pair_ref, mine_ref, theirs_ref, kv_weights, qo_weights, sems)
        pltpu.make_async_copy(theirs_ref, qo_weights, sems.at[1]).wait()

    dkv_ref, dquery_ref, *back_refs = refs[given:]
    count, lat, width = branch_ref.shape
    rows, cols = kv_ref.shape[1], kv_ref.shape[2] // 2
    branch = branch_ref[...].reshape(count * lat, width)
    all_mixed = product(branch, qo_weights[:, cols:]).astype(BF16)
    for image in range(count):
        keys, values = kv_ref[image, :, :cols], kv_ref[image, :, cols:]
        query = stacked(qm_ref[image, :, :cols], heads)
        probs = softmax_rows(product_right(query, keys))
        grad_mixed = stacked(all_mixed[image * lat : (image + 1) * lat], heads)
        grad_probs = product_right(grad_mixed, values)
        inner = jnp.sum(grad_probs * probs, axis=-1, keepdims=True)
        grad_scores = (probs * (grad_probs - inner)).astype(BF16)
        dquery_ref[image] = unstacked(product(grad_scores, keys), heads).astype(BF16)
        dkv_ref[image, :, :cols] = product_left(grad_scores, query).astype(BF16)
        dkv_ref[image, :, cols:] = product_left(probs.astype(BF16), grad_mixed).astype(BF16)

    @pl.when(pl.program_id(0) == 0)
    def _():
        pltpu.make_async_copy(mine_ref, kv_weights, sems.at[0]).wait()

    back = product_right(dkv_ref[...].reshape(count * rows, 2 * cols), kv_weights[...]).reshape(count, rows, width)
    extra = product_right(dquery_ref[...].reshape(count * lat, cols), qo_weights[:, :cols]) * scale
    extra = extra.reshape(count, lat, width)
    for index, back_ref in enumerate(back_refs):

        @pl.when(pl.program_id(0) == index // count)
        def _(back_ref=back_ref, image=index % count):
            back_ref[0, :patch] = back[image, :patch].astype(BF16)
            back_ref[0, patch:] = (back[image, patch:] + extra[image]).astype(BF16)


def attend_back(pair, mine, theirs, branch, kv, qm, heads, patch, first, steps, per, carried):
    total, rows, cols = kv.shape
    lat, width = branch.shape[1:]
    part = lambda *shape: pl.BlockSpec((per,) + shape, lambda i: (first - i, 0, 0))
    given = list(carried or ())
    dkv, dquery, *backs = pl.pallas_call(
        functools.partial(attend_back_kernel, heads, patch, HEAD ** (-0.5), len(given)),
        grid=(steps,),
        in_specs=[SMALL, ANY, ANY, part(lat, width), part(rows, cols), part(lat, cols)] + [ANY] * len(given),
        out_specs=[part(rows, cols), part(lat, cols // 2)] + [whole((1, rows, width))] * (steps * per),
        out_shape=[
            jax.ShapeDtypeStruct((total, rows, cols), BF16),
            jax.ShapeDtypeStruct((total, lat, cols // 2), BF16),
        ]
        + [jax.ShapeDtypeStruct((1, rows, width), BF16)] * (steps * per),
        scratch_shapes=weight_scratch(mine),
        input_output_aliases={6 + i: i for i in range(len(given))},
        compiler_params=pltpu.CompilerParams(vmem_limit_bytes=VMEM),
        cost_estimate=SOME,
    )(pair, mine, theirs, branch, kv, qm, *given)
    return dkv, dquery, backs


def feed_kernel(tile, parts, cot_ref, cot_other_ref, weights_ref, *refs):
    hidden_refs, refs = refs[:parts], refs[parts:]
    all_ref, cots_ref, active_ref, upper_ref, *part_refs, weights, total_ref, sem = refs
    cols = weights_ref.shape[1] // 2
    copy = pltpu.make_async_copy(weights_ref, weights, sem)
    copy.start()
    start = 0
    for hidden_ref in hidden_refs:
        all_ref[start : start + hidden_ref.shape[0]] = hidden_ref[...]
        start += hidden_ref.shape[0]
    cots_ref[: start // 2] = cot_ref[...]
    cots_ref[start // 2 :] = cot_other_ref[...]
    rows = all_ref.shape[0]
    block = math.gcd(rows, 256)
    copy.wait()
    for index in range(cols // tile):
        place = slice(index * tile, (index + 1) * tile)
        up, down = weights[:, place], weights[:, cols + index * tile : cols + (index + 1) * tile]
        for first in range(0, rows, block):
            here = slice(first, first + block)
            upper = product(all_ref[here], up)
            cdf = 0.5 * (1.0 + lax.erf(upper * (0.5**0.5)))
            slope = cdf + upper * jnp.exp(-0.5 * upper * upper) * (0.5 / math.pi) ** 0.5
            grad_upper = (slope * product(cots_ref[here], down)).astype(BF16)
            active_ref[here, place] = (upper * cdf).astype(BF16)
            upper_ref[here, place] = grad_upper
    for first in range(0, rows, block):
        here = slice(first, first + block)
        total_ref[here] = product_right(upper_ref[here], weights[:, :cols])
    start = 0
    for part_ref in part_refs:
        part_ref[...] = total_ref[start : start + part_ref.shape[0]].astype(BF16)
        start += part_ref.shape[0]


def feed(hidden, cot, cot_other, weights):
    width = cot.shape[1]
    rows = 2 * cot.shape[0]
    cols = weights.shape[1] // 2
    tile = 256 if cols % 256 == 0 else math.gcd(cols, 384)
    shapes = [(rows, width)] * 2 + [(rows, cols)] * 2 + [part.shape for part in hidden]
    return pl.pallas_call(
        functools.partial(feed_kernel, tile, len(hidden)),
        grid=(1,),
        in_specs=[whole(cot.shape)] * 2 + [ANY] + [whole(part.shape) for part in hidden],
        out_specs=[whole(shape) for shape in shapes],
        out_shape=[jax.ShapeDtypeStruct(shape, BF16) for shape in shapes],
        scratch_shapes=[pltpu.VMEM(weights.shape, BF16), pltpu.VMEM((rows, width), F32), pltpu.SemaphoreType.DMA],
        compiler_params=pltpu.CompilerParams(vmem_limit_bytes=MOST),
        cost_estimate=LITTLE,
    )(cot, cot_other, weights, *hidden)


def feed_out_kernel(active_ref, weights_ref, own_ref, other_ref):
    rows = own_ref.shape[0]
    own_ref[...] = product_right(active_ref[:rows], weights_ref[...]).astype(BF16)
    other_ref[...] = product_right(active_ref[rows:], weights_ref[...]).astype(BF16)


def feed_out(active, weights):
    rows, cols = active.shape
    width = weights.shape[0]
    return pl.pallas_call(
        feed_out_kernel,
        grid=(1,),
        in_specs=[whole(active.shape), pl.BlockSpec((width, cols), lambda i: (0, 1))],
        out_specs=[whole((rows // 2, width))] * 2,
        out_shape=[jax.ShapeDtypeStruct((rows // 2, width), BF16)] * 2,
        compiler_params=pltpu.CompilerParams(vmem_limit_bytes=VMEM),
        cost_estimate=LITTLE,
    )(active, weights)


def feed_grads_kernel(hidden_ref, cot_ref, upper_ref, active_ref, to_ref):
    half = upper_ref.shape[1]
    to_ref[:, :half] = product_left(hidden_ref[...], upper_ref[...]).astype(BF16)
    to_ref[:, half:] = product_left(cot_ref[...], active_ref[...]).astype(BF16)


def row_tiles(width):
    return width // math.gcd(width, 384)


def feed_grads(hidden, cot, upper, active):
    rows, width = hidden.shape
    cols = upper.shape[1]
    steps = row_tiles(width)
    left = pl.BlockSpec((rows, width // steps), lambda i: (0, i))
    right = pl.BlockSpec((rows, cols), lambda i: (0, 0))
    return pl.pallas_call(
        feed_grads_kernel,
        grid=(steps,),
        in_specs=[left, left, right, right],
        out_specs=pl.BlockSpec((width // steps, 2 * cols), lambda i: (i, 0)),
        out_shape=jax.ShapeDtypeStruct((width, 2 * cols), BF16),
        compiler_params=pltpu.CompilerParams(vmem_limit_bytes=MOST),
        cost_estimate=LITTLE,
    )(hidden, cot, upper, active)


def add_pieces_kernel(first_ref, *refs):
    *piece_refs, to_ref = refs
    rows = piece_refs[0].shape[0]
    for index, piece_ref in enumerate(piece_refs):
        place = slice(index * rows, (index + 1) * rows)
        to_ref[place] = (first_ref[place].astype(F32) + piece_ref[...].astype(F32)).astype(BF16)


def pick_kernel(*refs):
    *from_refs, to_ref = refs
    rows = from_refs[0].shape[1]
    for index, from_ref in enumerate(from_refs):
        to_ref[index * rows : (index + 1) * rows] = from_ref[0]


def pick(parts, block, rows):
    width = parts[0].shape[2]
    return pl.pallas_call(
        pick_kernel,
        grid=(1,),
        in_specs=[pl.BlockSpec((1, rows, width), lambda i: (0, block, 0))] * len(parts),
        out_specs=pl.BlockSpec((len(parts) * rows, width), lambda i: (0, 0)),
        out_shape=jax.ShapeDtypeStruct((len(parts) * rows, width), BF16),
        compiler_params=pltpu.CompilerParams(vmem_limit_bytes=VMEM),
        cost_estimate=LITTLE,
    )(*parts)


def attend_grads_kernel(patch, scale, pair_ref, joined_ref, branch_ref, dkv_ref, dquery_ref, qm_ref, keep_ref, *give_refs):
    count, rows, tile = joined_ref.shape
    lat, cols = rows - patch, dquery_ref.shape[2]
    joined = joined_ref[...].reshape(count * rows, tile)
    latent = joined_ref[:, patch:].reshape(count * lat, tile)
    kv = product_left(joined, dkv_ref[...].reshape(count * rows, 2 * cols)).astype(BF16)
    query = (product_left(latent, dquery_ref[...].reshape(count * lat, cols)) * scale).astype(BF16)
    out = product_left(branch_ref[...], qm_ref[:, :, cols:].reshape(count * lat, cols)).astype(BF16)

    @pl.when(pair_ref[0] == 0)
    def _():
        keep_ref[...] = kv

    @pl.when(pair_ref[0] == 1)
    def _():
        keep_ref[:, :cols] = query
        keep_ref[:, cols:] = out

    for step, give_ref in enumerate(give_refs):

        @pl.when((pl.program_id(0) == step) & (pair_ref[0] == 0))
        def _(give_ref=give_ref):
            give_ref[:, :cols] = query
            give_ref[:, cols:] = out

        @pl.when((pl.program_id(0) == step) & (pair_ref[0] == 1))
        def _(give_ref=give_ref):
            give_ref[...] = kv


def attend_grads(pair, joined, branch, dkv, dquery, qm, patch):
    total, rows, width = joined.shape
    lat, cols = rows - patch, dkv.shape[2]
    steps = row_tiles(width)
    tile = pl.BlockSpec((width // steps, cols), lambda i: (i, 0))
    return pl.pallas_call(
        functools.partial(attend_grads_kernel, patch, HEAD ** (-0.5)),
        grid=(steps,),
        in_specs=[
            SMALL,
            pl.BlockSpec((total, rows, width // steps), lambda i: (0, 0, i)),
            pl.BlockSpec((total * lat, width // steps), lambda i: (0, i)),
            whole(dkv.shape), whole(dquery.shape), whole(qm.shape),
        ],
        out_specs=[tile] + [whole((width // steps, cols))] * steps,
        out_shape=[jax.ShapeDtypeStruct((width, cols), BF16)] + [jax.ShapeDtypeStruct((width // steps, cols), BF16)] * steps,
        compiler_params=pltpu.CompilerParams(vmem_limit_bytes=VMEM),
        cost_estimate=LITTLE,
    )(pair, joined, branch, dkv, dquery, qm)


def whole(shape):
    return pl.BlockSpec(shape, lambda *_: (0,) * len(shape))


def once(kernel, operands, shapes, cost=LITTLE, limit=VMEM):
    return pl.pallas_call(
        kernel,
        grid=(1,),
        in_specs=[whole(operand.shape) for operand in operands],
        out_specs=[whole(shape) for shape, _ in shapes],
        out_shape=[jax.ShapeDtypeStruct(shape, kind) for shape, kind in shapes],
        compiler_params=pltpu.CompilerParams(vmem_limit_bytes=limit),
        cost_estimate=cost,
    )(*operands)


def attended_kernel(small_ref, latent_ref, *refs):
    *part_refs, attended_ref, hidden_ref = refs
    images = latent_ref.shape[0]
    each = len(part_refs) // images
    for image in range(images):
        total = latent_ref[image].astype(F32)
        for part_ref in part_refs[image * each : (image + 1) * each]:
            total = total + part_ref[0].astype(F32)
        attended_ref[image] = total
        hidden_ref[image] = normed(total, small_ref[0, 2:3], small_ref[1, 2:3]).astype(BF16)


def summed_kernel(other_ref, *refs):
    count = len(refs) // 2
    rows = other_ref.shape[0] // count
    for index in range(count):
        other = other_ref[index * rows : (index + 1) * rows].astype(F32)
        refs[count + index][...] = (refs[index][...].astype(F32) + other).astype(BF16)


def through_kernel(*refs):
    for index in range(2):
        left_ref, right_ref, to_ref = refs[2 * index], refs[2 * index + 1], refs[4 + index]
        to_ref[...] = (left_ref[...].astype(F32) + right_ref[...].astype(F32)).astype(BF16)


def norm_back(rows, gain, grad):
    average = jnp.mean(rows, axis=-1, keepdims=True)
    centred = rows - average
    inverse = lax.rsqrt(jnp.mean(centred * centred, axis=-1, keepdims=True) + EPSILON)
    unit = centred * inverse
    scaled = grad * gain
    first = jnp.mean(scaled, axis=-1, keepdims=True)
    second = jnp.mean(scaled * unit, axis=-1, keepdims=True)
    back = inverse * (scaled - first - unit * second)
    return back, jnp.sum(grad * unit, axis=0, keepdims=True), jnp.sum(grad, axis=0, keepdims=True)


def branch_kernel(small_ref, attended_ref, cot_ref, *refs):
    *part_refs, grad_ref, branch_ref, sums_ref = refs
    images, lat, width = attended_ref.shape
    grad = sum(part_ref[...].astype(F32) for part_ref in part_refs)
    back, gain, bias = norm_back(attended_ref[...].reshape(images * lat, width), small_ref[0, 2:3], grad)
    total = (cot_ref[...].reshape(images * lat, width).astype(F32) + back).reshape(images, lat, width)
    grad_ref[...] = total
    branch_ref[...] = total.astype(BF16)
    sums_ref[0:1] = gain
    sums_ref[1:2] = bias


def rows_back_kernel(small_ref, sums_two_ref, media_ref, latent_ref, grad_ref, *refs):
    *part_refs, media_to_ref, latent_to_ref, sums_ref = refs
    images, patch, _ = media_ref.shape
    each = len(part_refs) // images
    totals = None
    for image in range(images):
        parts = part_refs[image * each : (image + 1) * each]
        grad = sum(part_ref[0, :patch].astype(F32) for part_ref in parts)
        media, gain_zero, bias_zero = norm_back(media_ref[image].astype(F32), small_ref[0, 0:1], grad)
        media_to_ref[image] = media
        grad = sum(part_ref[0, patch:].astype(F32) for part_ref in parts)
        latent, gain_one, bias_one = norm_back(latent_ref[image].astype(F32), small_ref[0, 1:2], grad)
        latent_to_ref[image] = grad_ref[image] + latent
        terms = gain_zero, gain_one, bias_zero, bias_one
        totals = terms if totals is None else [left + right for left, right in zip(totals, terms)]
    for row, total in zip((0, 1, 3, 4), totals):
        sums_ref[row : row + 1] = total
    sums_ref[2:3] = sums_two_ref[0:1]
    sums_ref[5:6] = sums_two_ref[1:2]


def in_thirds(values):
    parts, rest = [], values
    for _ in range(3):
        part = lax.reduce_precision(rest, exponent_bits=8, mantissa_bits=7)
        parts.append(part.astype(BF16))
        rest = rest - part
    return jnp.stack(parts)


def local(media_features, latents, cotangent, image_counts, w_query, w_key, w_value, w_out, w_up, w_down,
          norm_gains, norm_biases):
    devices_x, devices_y = lax.axis_size("gx"), lax.axis_size("gy")
    masks = far_masks()
    img_count, lat, width = latents.shape
    patch = media_features.shape[1]
    rows = patch + lat
    shard = w_query.shape[0]
    head_width = width // devices_y
    heads = 2 * head_width // HEAD
    pair = (lax.axis_index("gy") % 2).astype(jnp.int32).reshape(1)
    ff_width = w_up.shape[1] // devices_y
    total = img_count * len(masks)

    four_width = 4 * head_width
    small = in_thirds(jnp.stack([norm_gains, norm_biases])).reshape(-1)
    extra = -(-small.size // (16 * four_width)) * 16
    small = jnp.pad(small, (0, extra * four_width - small.size)).reshape(extra, four_width)
    four = regroup(small, devices_y, w_key, w_value, w_query, w_out.T)
    four = lax.all_to_all(four, "gy", split_axis=0, concat_axis=0, tiled=True)
    mine = lax.all_gather(four[:, extra:].reshape(devices_y * shard, four_width), "gx", axis=0, tiled=True)

    two = jnp.concatenate(
        [part.reshape(shard, devices_y, ff_width).transpose(1, 0, 2) for part in (w_up, w_down.T)], axis=2
    )
    two, four = tie(two, four)
    small = four[:, :extra].reshape(devices_y, -1)[:, : 18 * shard].reshape(devices_y, 3, 6 * shard)
    small = gather_small(jnp.sum(small.astype(F32), axis=1).reshape(1, -1), "gx")
    small = small.reshape(devices_x, devices_y, 6, shard).transpose(2, 0, 1, 3).reshape(2, 3, width)

    two = lax.all_to_all(two, "gy", split_axis=0, concat_axis=0, tiled=True)
    live = (jnp.arange(img_count, dtype=jnp.int32) < image_counts[0]).astype(BF16)
    cot_own = cotangent * live[:, None, None]
    own = [
        jnp.concatenate([part[i : i + 1] for part in (media_features, latents, cot_own)], axis=1) for i in range(img_count)
    ]
    two, small, *own = tie(two, small, *own)
    ff_rows = two.reshape(devices_y * shard, 2 * ff_width)
    gains, biases = small[0], small[1]

    raw = {(0, i): own[i] for i in range(img_count)}
    if len(masks) == 4 and img_count == 2:
        slots = [(0, 0), (0, 1), (2, 0), (4, 0), (2, 1), (4, 1), (6, 0), (6, 1)]
        raw[2, 0], raw[4, 0], later = tie(swap(own[0], 2), swap(own[0], 4), own[1])
        raw[2, 0], raw[4, 0], ff_rows, mine = tie(raw[2, 0], raw[4, 0], ff_rows, mine)
        raw[2, 1], raw[4, 1], raw[6, 0] = swap(later, 2), swap(later, 4), swap(raw[2, 0], 4)
    else:
        slots = [(mask, i) for mask in masks for i in range(img_count)]
        for mask in masks[1:]:
            raw.update({(mask, i): swap(own[i], mask) for i in range(img_count)})
    ff_mine = lax.all_gather(ff_rows, "gx", axis=0, tiled=True)
    theirs = swap(mine, 1)

    steps, carried, out_parts = total // img_count, None, {}
    for step in range(steps):
        here = slots[step * img_count : (step + 1) * img_count]
        if carried:
            carried[0], *raws = tie(carried[0], *[raw[slot] for slot in here])
            raw.update(dict(zip(here, raws)))
        if (4, 1) in here and (6, 1) not in raw:
            raw[6, 1] = swap(raw[4, 1], 2)
        *carried, first_part, second_part = attend(
            pair, mine, theirs, small, [raw[slot] for slot in here], heads, patch, rows, step, total, carried
        )
        out_parts.update(dict(zip(here, (first_part, second_part))))
    joined_all, kv_all, qm_all = carried

    qm_all, *parts = tie(qm_all, *[raw[mask, i] for mask in masks for i in range(img_count)])
    cot_own_all = pick(parts, rows // lat, lat)
    out_parts = [
        swap(out_parts[mask, i], mask) if mask else out_parts[mask, i] for i in range(img_count) for mask in masks
    ]
    like_latents = lambda kind: (latents.shape, kind)
    attended, hidden_own = once(
        attended_kernel, [small, latents, *out_parts], [like_latents(F32), like_latents(BF16)]
    )
    hidden_own, cot_own_all = tie(hidden_own, cot_own_all)
    cot_other = swap(cot_own_all, 1)
    hidden = [part.reshape(img_count * lat, width) for part in spread(hidden_own).values()]
    hidden.append(swap(jnp.concatenate(hidden), 1))

    def plus(left, right):
        return (left.astype(F32) + right.astype(F32)).astype(BF16)

    def collect_pairs(parts):
        parts = [part.reshape(img_count, lat, width) for part in parts]
        return [parts[0]] + [swap(part, mask) for mask, part in zip(masks[1:], parts[1:])]

    total_of = lambda parts: sum(part.astype(F32) for part in parts)

    def summed(parts, other):
        return once(summed_kernel, [swap(other, 1), *parts], [(part.shape, BF16) for part in parts], limit=MOST)

    hidden, cot_all, active, grad_upper, *hidden_parts, hidden_other = feed(hidden, cot_own_all, cot_other, ff_mine)
    hidden_parts = summed(hidden_parts, hidden_other)
    grad_upper, *hidden_parts = tie(grad_upper, *hidden_parts)
    ff_grads = feed_grads(hidden, cot_all, grad_upper, active)
    ff_part = lax.psum_scatter(ff_grads, "gx", scatter_dimension=0, tiled=True)
    hidden_parts = collect_pairs(hidden_parts)
    hidden_parts = [part.reshape(img_count * lat, width) for part in hidden_parts]
    grad_attended, grad_branch, sums_two = once(
        branch_kernel, [small, attended, cot_own, *hidden_parts],
        [like_latents(F32), like_latents(BF16), ((2, width), F32)], limit=MOST,
    )
    branch = spread(grad_branch)
    ffn_parts = feed_out(active, ff_mine)
    *branch, ffn_part, ffn_other = tie(*branch.values(), *ffn_parts)
    branch = jnp.concatenate([branch[masks.index(mask)][i : i + 1] for mask, i in slots])

    arrays = pair, mine, theirs, branch, kv_all, qm_all, heads, patch
    back, carried, step = {}, None, steps - 1
    for count in (1, steps - 1):
        *carried, results = attend_back(*arrays, step, count, img_count, carried)
        for index, part in enumerate(results):
            back[slots[(step - index // img_count) * img_count + index % img_count]] = part
        step -= count
    dkv_all, dquery_all = carried

    if len(masks) == 4 and img_count == 2:
        last = swap(back[6, 0], 4), swap(back[6, 1], 2)
        through = once(
            through_kernel, [back[2, 0], last[0], back[4, 1], last[1]], [(back[2, 0].shape, BF16)] * 2
        )
        dkv_all, *through = tie(dkv_all, *through)
    def home(part):
        return lax.all_to_all(part.reshape(devices_y, shard, -1), "gy", split_axis=0, concat_axis=0, tiled=True)

    keep, *give = attend_grads(
        pair, joined_all, branch.reshape(total * lat, width), dkv_all, dquery_all, qm_all, patch
    )
    if len(masks) == 4 and img_count == 2:
        keep, ff_part, *through = tie(keep, ff_part, swap(through[0], 2), swap(through[1], 4), back[4, 0], back[2, 1])
        direct = swap(through[2], 4), swap(through[3], 2)
        arrived = [back[0, 0], through[0], direct[0], back[0, 1], direct[1], through[1]]
    else:
        arrived = [swap(back[mask, i], mask) if mask else back[mask, i] for i in range(img_count) for mask in masks]
    give = [swap(part, 1) for part in give]
    (at_grads,) = once(add_pieces_kernel, [keep, *give], [(keep.shape, BF16)])
    at_grads, ffn_other = tie(at_grads, ffn_other)
    shares = lax.psum_scatter(at_grads, "gx", scatter_dimension=0, tiled=True)
    ffn_part = ffn_part.reshape(len(masks), img_count * lat, width)
    ffn_parts = summed([ffn_part[i] for i in range(len(masks))], ffn_other)

    each = len(arrived)
    *arrived, ff_part = tie(*arrived, *ffn_parts, ff_part)
    arrived, ffn_parts = arrived[:each], arrived[each:]
    grad_media, grad_latents, sums = once(
        rows_back_kernel, [small, sums_two, media_features, latents, grad_attended, *arrived],
        [(media_features.shape, F32), like_latents(F32), ((6, width), F32)],
        cost=SOME, limit=MOST,
    )
    sums = sums + swap(sums, 1)
    sums = sum([sums] + [swap(sums, mask) for mask in masks[1:]])
    sums, *ffn_parts = tie(sums, *ffn_parts)
    ffn_parts = collect_pairs(ffn_parts)
    sums = sum([sums] + [swap(sums, mask, "gx") for mask in range(1, devices_x)])
    place = lax.axis_index("gx") * devices_y + lax.axis_index("gy")
    sums = lax.dynamic_slice_in_dim(sums, place * shard, shard, axis=1)

    shares, sums, ff_part, *ffn_parts = tie(shares, sums, home(ff_part), *ffn_parts)
    grad_key, grad_value, grad_query, grad_out = ungroup(home(shares), 4, True)
    outputs = ((attended + total_of(ffn_parts)) * live.astype(F32)[:, None, None]).astype(BF16)
    grad_up, grad_down = ungroup(ff_part, 2, False)
    grad_down = grad_down.T
    return (
        outputs, grad_media, grad_latents, grad_query, grad_key, grad_value, grad_out.T, grad_up, grad_down,
        sums[:3], sums[3:],
    )


def solution(mesh):
    split = ("gx", "gy")
    images, first, second = P(split, None, None), P(split, None), P(None, split)
    return jax.shard_map(
        local,
        mesh=mesh,
        in_specs=(images, images, images, P(split), first, first, first, second, first, second, second, second),
        out_specs=(images, images, images, first, first, first, second, first, second, second, second),
        check_vma=False,
    )
```

```python
import functools
import math

import jax
import jax.numpy as jnp
from jax import lax
from jax.experimental import pallas as pl
from jax.experimental.pallas import tpu as pltpu
from jax.sharding import PartitionSpec as P

HEAD = 96
EPSILON = 1e-05
BF16 = jnp.bfloat16
F32 = jnp.float32
VMEM = 24 * 2**20
MOST = 56 * 2**20
SOME = pl.CostEstimate(flops=26 * 10**9, bytes_accessed=1024, transcendentals=0)
LITTLE = pl.CostEstimate(flops=1024, bytes_accessed=1024, transcendentals=0)


def product(left, right):
    return jnp.dot(left, right, preferred_element_type=F32)


def product_left(left, right):
    return lax.dot_general(left, right, (((0,), (0,)), ((), ())), preferred_element_type=F32)


def product_right(left, right):
    return lax.dot_general(left, right, (((1,), (1,)), ((), ())), preferred_element_type=F32)


def tie(*values):
    return lax.optimization_barrier(values)


def swap(block, mask, axis="gy"):
    count = lax.axis_size(axis)
    return lax.ppermute(block, axis, [(i, i ^ mask) for i in range(count)])


def far_masks():
    return [mask for mask in range(lax.axis_size("gy")) if mask % 2 == 0]


def spread(block):
    return {mask: swap(block, mask) if mask else block for mask in far_masks()}


def regroup_kernel(first_ref, *refs):
    *from_refs, to_ref = refs
    extra, half = first_ref.shape[0], len(from_refs) // 2
    groups = to_ref.shape[0] // 2
    cols = from_refs[0].shape[1] // groups
    for device in range(2 * groups):
        group, core = device // 2, device % 2
        to_ref[device, :extra] = first_ref[...]
        for index, from_ref in enumerate(from_refs[core * half : (core + 1) * half]):
            to_ref[device, extra:, index * cols : (index + 1) * cols] = from_ref[:, group * cols : (group + 1) * cols]


def regroup(first, devices, *weights):
    shard, width = weights[0].shape
    return pl.pallas_call(
        regroup_kernel,
        out_shape=jax.ShapeDtypeStruct((devices, first.shape[0] + shard, first.shape[1]), BF16),
        compiler_params=pltpu.CompilerParams(vmem_limit_bytes=MOST),
        cost_estimate=LITTLE,
    )(first, *weights)


def ungroup_kernel(by_pair, from_ref, *to_refs):
    devices, _, width = from_ref.shape
    per = len(to_refs) // 2 if by_pair else len(to_refs)
    cols = width // per
    for index, to_ref in enumerate(to_refs):
        sources = range(index // per, devices, 2) if by_pair else range(devices)
        place = slice(index % per * cols, (index % per + 1) * cols)
        for position, device in enumerate(sources):
            to_ref[:, position * cols : (position + 1) * cols] = from_ref[device, :, place].astype(F32)


def ungroup(blocks, count, by_pair, cost=LITTLE):
    devices, shard, width = blocks.shape
    return pl.pallas_call(
        functools.partial(ungroup_kernel, by_pair),
        out_shape=[jax.ShapeDtypeStruct((shard, devices * width // count), F32)] * count,
        compiler_params=pltpu.CompilerParams(vmem_limit_bytes=VMEM),
        cost_estimate=cost,
    )(blocks)


def bits_of(count):
    bits, bit = [], 1
    while bit < count:
        bits.append(bit)
        bit *= 2
    return bits


def gather_small(rows, axis):
    place = lax.axis_index(axis)
    for bit in bits_of(lax.axis_size(axis)):
        other = swap(rows, bit, axis)
        upper = (place & bit) != 0
        rows = jnp.concatenate([jnp.where(upper, other, rows), jnp.where(upper, rows, other)])
    return rows


def normed(rows, gain, bias):
    average = jnp.mean(rows, axis=-1, keepdims=True)
    centred = rows - average
    spread_of = jnp.mean(centred * centred, axis=-1, keepdims=True)
    return centred * lax.rsqrt(spread_of + EPSILON) * gain + bias


def head_mask(rows, lanes, head):
    lane = lax.broadcasted_iota(jnp.int32, (rows, lanes), 1)
    return (lane >= head * HEAD) & (lane < (head + 1) * HEAD)


def stacked(rows, heads):
    count, lanes = rows.shape
    return jnp.concatenate(
        [jnp.where(head_mask(count, lanes, h), rows, jnp.zeros_like(rows)) for h in range(heads)]
    )


def unstacked(rows, heads):
    count, lanes = rows.shape[0] // heads, rows.shape[1]
    total = rows[:count]
    for h in range(1, heads):
        total = jnp.where(head_mask(count, lanes, h), rows[h * count : (h + 1) * count], total)
    return total


def softmax_rows(scores):
    top = jnp.max(scores, axis=-1, keepdims=True)
    raised = jnp.exp(scores - top)
    return raised / jnp.sum(raised, axis=-1, keepdims=True)


def load_weights(pair_ref, mine_ref, theirs_ref, kv_weights, qo_weights, sems):
    @pl.when(pair_ref[0] == 0)
    def _():
        pltpu.make_async_copy(theirs_ref, qo_weights, sems.at[1]).start()
        pltpu.make_async_copy(mine_ref, kv_weights, sems.at[0]).start()

    @pl.when(pair_ref[0] == 1)
    def _():
        pltpu.make_async_copy(mine_ref, qo_weights, sems.at[1]).start()
        pltpu.make_async_copy(theirs_ref, kv_weights, sems.at[0]).start()


def attend_kernel(heads, patch, scale, raws, given, pair_ref, mine_ref, theirs_ref, small_ref, *refs):
    *refs, kv_weights, qo_weights, sems = refs
    joined_ref, kv_ref, qm_ref, *out_refs = refs[raws + given :]
    count, rows, width = joined_ref.shape
    load_weights(pair_ref, mine_ref, theirs_ref, kv_weights, qo_weights, sems)
    for image, raw_ref in enumerate(refs[:raws]):
        media = normed(raw_ref[0, :patch].astype(F32), small_ref[0, 0:1], small_ref[1, 0:1])
        latent = normed(raw_ref[0, patch:rows].astype(F32), small_ref[0, 1:2], small_ref[1, 1:2])
        joined_ref[image, :patch] = media.astype(BF16)
        joined_ref[image, patch:] = latent.astype(BF16)
    pltpu.make_async_copy(mine_ref, kv_weights, sems.at[0]).wait()
    pltpu.make_async_copy(theirs_ref, qo_weights, sems.at[1]).wait()
    lat, cols = rows - patch, kv_weights.shape[1] // 2
    joined = joined_ref[...].reshape(count * rows, width)
    latent = joined_ref[:, patch:].reshape(count * lat, width)
    kv_ref[...] = product(joined, kv_weights[...]).astype(BF16).reshape(count, rows, 2 * cols)
    query = (product(latent, qo_weights[:, :cols]) * scale).astype(BF16)
    qm_ref[:, :, :cols] = query.reshape(count, lat, cols)
    mixed = []
    for image in range(count):
        probs = softmax_rows(product_right(stacked(query[image * lat : (image + 1) * lat], heads), kv_ref[image, :, :cols]))
        mixed.append(unstacked(product(probs.astype(BF16), kv_ref[image, :, cols:]), heads).astype(BF16))
    mixed = jnp.concatenate(mixed)
    qm_ref[:, :, cols:] = mixed.reshape(count, lat, cols)
    total = product_right(mixed, qo_weights[:, cols:]).astype(BF16).reshape(count, lat, width)
    for image, out_ref in enumerate(out_refs):
        out_ref[0] = total[image]


SMALL = pl.BlockSpec(memory_space=pltpu.SMEM)
ANY = pl.BlockSpec(memory_space=pl.ANY)


def weight_scratch(mine):
    return [pltpu.VMEM(mine.shape, BF16)] * 2 + [pltpu.SemaphoreType.DMA((2,))]


def attend(pair, mine, theirs, small, raws, heads, patch, rows, step, total, carried):
    width, cols = mine.shape
    lat, per = rows - patch, len(raws)
    part = lambda *shape: pl.BlockSpec((per,) + shape, lambda i: (step, 0, 0))
    given = list(carried or ())
    return pl.pallas_call(
        functools.partial(attend_kernel, heads, patch, HEAD ** (-0.5), per, len(given)),
        grid=(1,),
        in_specs=[SMALL, ANY, ANY, whole(small.shape)] + [whole(raw.shape) for raw in raws] + [ANY] * len(given),
        out_specs=[part(rows, width), part(rows, cols), part(lat, cols)] + [whole((1, lat, width))] * per,
        out_shape=[
            jax.ShapeDtypeStruct((total, rows, width), BF16),
            jax.ShapeDtypeStruct((total, rows, cols), BF16),
            jax.ShapeDtypeStruct((total, lat, cols), BF16),
        ]
        + [jax.ShapeDtypeStruct((1, lat, width), BF16)] * per,
        scratch_shapes=weight_scratch(mine),
        input_output_aliases={4 + per + i: i for i in range(len(given))},
        compiler_params=pltpu.CompilerParams(vmem_limit_bytes=VMEM),
        cost_estimate=LITTLE,
    )(pair, mine, theirs, small, *raws, *given)


def attend_back_kernel(heads, patch, scale, given, pair_ref, mine_ref, theirs_ref, branch_ref, kv_ref, qm_ref, *refs):
    *refs, kv_weights, qo_weights, sems = refs

    @pl.when(pl.program_id(0) == 0)
    def _():
        load_weights(pair_ref, mine_ref, theirs_ref, kv_weights, qo_weights, sems)
        pltpu.make_async_copy(theirs_ref, qo_weights, sems.at[1]).wait()

    dkv_ref, dquery_ref, *back_refs = refs[given:]
    count, lat, width = branch_ref.shape
    rows, cols = kv_ref.shape[1], kv_ref.shape[2] // 2
    branch = branch_ref[...].reshape(count * lat, width)
    all_mixed = product(branch, qo_weights[:, cols:]).astype(BF16)
    for image in range(count):
        keys, values = kv_ref[image, :, :cols], kv_ref[image, :, cols:]
        query = stacked(qm_ref[image, :, :cols], heads)
        probs = softmax_rows(product_right(query, keys))
        grad_mixed = stacked(all_mixed[image * lat : (image + 1) * lat], heads)
        grad_probs = product_right(grad_mixed, values)
        inner = jnp.sum(grad_probs * probs, axis=-1, keepdims=True)
        grad_scores = (probs * (grad_probs - inner)).astype(BF16)
        dquery_ref[image] = unstacked(product(grad_scores, keys), heads).astype(BF16)
        dkv_ref[image, :, :cols] = product_left(grad_scores, query).astype(BF16)
        dkv_ref[image, :, cols:] = product_left(probs.astype(BF16), grad_mixed).astype(BF16)

    @pl.when(pl.program_id(0) == 0)
    def _():
        pltpu.make_async_copy(mine_ref, kv_weights, sems.at[0]).wait()

    back = product_right(dkv_ref[...].reshape(count * rows, 2 * cols), kv_weights[...]).reshape(count, rows, width)
    extra = product_right(dquery_ref[...].reshape(count * lat, cols), qo_weights[:, :cols]) * scale
    extra = extra.reshape(count, lat, width)
    for index, back_ref in enumerate(back_refs):

        @pl.when(pl.program_id(0) == index // count)
        def _(back_ref=back_ref, image=index % count):
            back_ref[0, :patch] = back[image, :patch].astype(BF16)
            back_ref[0, patch:] = (back[image, patch:] + extra[image]).astype(BF16)


def attend_back(pair, mine, theirs, branch, kv, qm, heads, patch, first, steps, per, carried):
    total, rows, cols = kv.shape
    lat, width = branch.shape[1:]
    part = lambda *shape: pl.BlockSpec((per,) + shape, lambda i: (first - i, 0, 0))
    given = list(carried or ())
    dkv, dquery, *backs = pl.pallas_call(
        functools.partial(attend_back_kernel, heads, patch, HEAD ** (-0.5), len(given)),
        grid=(steps,),
        in_specs=[SMALL, ANY, ANY, part(lat, width), part(rows, cols), part(lat, cols)] + [ANY] * len(given),
        out_specs=[part(rows, cols), part(lat, cols // 2)] + [whole((1, rows, width))] * (steps * per),
        out_shape=[
            jax.ShapeDtypeStruct((total, rows, cols), BF16),
            jax.ShapeDtypeStruct((total, lat, cols // 2), BF16),
        ]
        + [jax.ShapeDtypeStruct((1, rows, width), BF16)] * (steps * per),
        scratch_shapes=weight_scratch(mine),
        input_output_aliases={6 + i: i for i in range(len(given))},
        compiler_params=pltpu.CompilerParams(vmem_limit_bytes=VMEM),
        cost_estimate=SOME,
    )(pair, mine, theirs, branch, kv, qm, *given)
    return dkv, dquery, backs


def feed_kernel(tile, parts, cot_ref, cot_other_ref, weights_ref, *refs):
    hidden_refs, refs = refs[:parts], refs[parts:]
    all_ref, cots_ref, active_ref, upper_ref, *part_refs, weights, total_ref, sem = refs
    cols = weights_ref.shape[1] // 2
    copy = pltpu.make_async_copy(weights_ref, weights, sem)
    copy.start()
    start = 0
    for hidden_ref in hidden_refs:
        all_ref[start : start + hidden_ref.shape[0]] = hidden_ref[...]
        start += hidden_ref.shape[0]
    cots_ref[: start // 2] = cot_ref[...]
    cots_ref[start // 2 :] = cot_other_ref[...]
    rows = all_ref.shape[0]
    block = math.gcd(rows, 256)
    copy.wait()
    for index in range(cols // tile):
        place = slice(index * tile, (index + 1) * tile)
        up, down = weights[:, place], weights[:, cols + index * tile : cols + (index + 1) * tile]
        for first in range(0, rows, block):
            here = slice(first, first + block)
            upper = product(all_ref[here], up)
            cdf = 0.5 * (1.0 + lax.erf(upper * (0.5**0.5)))
            slope = cdf + upper * jnp.exp(-0.5 * upper * upper) * (0.5 / math.pi) ** 0.5
            grad_upper = (slope * product(cots_ref[here], down)).astype(BF16)
            active_ref[here, place] = (upper * cdf).astype(BF16)
            upper_ref[here, place] = grad_upper
    for first in range(0, rows, block):
        here = slice(first, first + block)
        total_ref[here] = product_right(upper_ref[here], weights[:, :cols])
    start = 0
    for part_ref in part_refs:
        part_ref[...] = total_ref[start : start + part_ref.shape[0]].astype(BF16)
        start += part_ref.shape[0]


def feed(hidden, cot, cot_other, weights):
    width = cot.shape[1]
    rows = 2 * cot.shape[0]
    cols = weights.shape[1] // 2
    tile = 256 if cols % 256 == 0 else math.gcd(cols, 384)
    shapes = [(rows, width)] * 2 + [(rows, cols)] * 2 + [(rows // 2, width)] * 2
    return pl.pallas_call(
        functools.partial(feed_kernel, tile, len(hidden)),
        grid=(1,),
        in_specs=[whole(cot.shape)] * 2 + [ANY] + [whole(part.shape) for part in hidden],
        out_specs=[whole(shape) for shape in shapes],
        out_shape=[jax.ShapeDtypeStruct(shape, BF16) for shape in shapes],
        scratch_shapes=[pltpu.VMEM(weights.shape, BF16), pltpu.VMEM((rows, width), F32), pltpu.SemaphoreType.DMA],
        compiler_params=pltpu.CompilerParams(vmem_limit_bytes=MOST),
        cost_estimate=LITTLE,
    )(cot, cot_other, weights, *hidden)


def feed_out_kernel(active_ref, weights_ref, own_ref, other_ref):
    rows = own_ref.shape[0]
    own_ref[...] = product_right(active_ref[:rows], weights_ref[...]).astype(BF16)
    other_ref[...] = product_right(active_ref[rows:], weights_ref[...]).astype(BF16)


def feed_out(active, weights):
    rows, cols = active.shape
    width = weights.shape[0]
    return pl.pallas_call(
        feed_out_kernel,
        grid=(1,),
        in_specs=[whole(active.shape), pl.BlockSpec((width, cols), lambda i: (0, 1))],
        out_specs=[whole((rows // 2, width))] * 2,
        out_shape=[jax.ShapeDtypeStruct((rows // 2, width), BF16)] * 2,
        compiler_params=pltpu.CompilerParams(vmem_limit_bytes=VMEM),
        cost_estimate=LITTLE,
    )(active, weights)


def feed_grads_kernel(hidden_ref, cot_ref, upper_ref, active_ref, to_ref):
    half = upper_ref.shape[1]
    to_ref[:, :half] = product_left(hidden_ref[...], upper_ref[...]).astype(BF16)
    to_ref[:, half:] = product_left(cot_ref[...], active_ref[...]).astype(BF16)


def row_tiles(width):
    return width // math.gcd(width, 384)


def feed_grads(hidden, cot, upper, active):
    rows, width = hidden.shape
    cols = upper.shape[1]
    steps = row_tiles(width)
    left = pl.BlockSpec((rows, width // steps), lambda i: (0, i))
    right = pl.BlockSpec((rows, cols), lambda i: (0, 0))
    return pl.pallas_call(
        feed_grads_kernel,
        grid=(steps,),
        in_specs=[left, left, right, right],
        out_specs=pl.BlockSpec((width // steps, 2 * cols), lambda i: (i, 0)),
        out_shape=jax.ShapeDtypeStruct((width, 2 * cols), BF16),
        compiler_params=pltpu.CompilerParams(vmem_limit_bytes=MOST),
        cost_estimate=LITTLE,
    )(hidden, cot, upper, active)


def add_pieces_kernel(first_ref, *refs):
    *piece_refs, to_ref = refs
    rows = piece_refs[0].shape[0]
    for index, piece_ref in enumerate(piece_refs):
        place = slice(index * rows, (index + 1) * rows)
        to_ref[place] = (first_ref[place].astype(F32) + piece_ref[...].astype(F32)).astype(BF16)


def pick_kernel(*refs):
    *from_refs, to_ref = refs
    rows = from_refs[0].shape[1]
    for index, from_ref in enumerate(from_refs):
        to_ref[index * rows : (index + 1) * rows] = from_ref[0]


def pick(parts, block, rows):
    width = parts[0].shape[2]
    return pl.pallas_call(
        pick_kernel,
        grid=(1,),
        in_specs=[pl.BlockSpec((1, rows, width), lambda i: (0, block, 0))] * len(parts),
        out_specs=pl.BlockSpec((len(parts) * rows, width), lambda i: (0, 0)),
        out_shape=jax.ShapeDtypeStruct((len(parts) * rows, width), BF16),
        compiler_params=pltpu.CompilerParams(vmem_limit_bytes=VMEM),
        cost_estimate=LITTLE,
    )(*parts)


def attend_grads_kernel(patch, scale, pair_ref, joined_ref, branch_ref, dkv_ref, dquery_ref, qm_ref, keep_ref, *give_refs):
    count, rows, tile = joined_ref.shape
    lat, cols = rows - patch, dquery_ref.shape[2]
    joined = joined_ref[...].reshape(count * rows, tile)
    latent = joined_ref[:, patch:].reshape(count * lat, tile)
    kv = product_left(joined, dkv_ref[...].reshape(count * rows, 2 * cols)).astype(BF16)
    query = (product_left(latent, dquery_ref[...].reshape(count * lat, cols)) * scale).astype(BF16)
    out = product_left(branch_ref[...], qm_ref[:, :, cols:].reshape(count * lat, cols)).astype(BF16)

    @pl.when(pair_ref[0] == 0)
    def _():
        keep_ref[...] = kv

    @pl.when(pair_ref[0] == 1)
    def _():
        keep_ref[:, :cols] = query
        keep_ref[:, cols:] = out

    for step, give_ref in enumerate(give_refs):

        @pl.when((pl.program_id(0) == step) & (pair_ref[0] == 0))
        def _(give_ref=give_ref):
            give_ref[:, :cols] = query
            give_ref[:, cols:] = out

        @pl.when((pl.program_id(0) == step) & (pair_ref[0] == 1))
        def _(give_ref=give_ref):
            give_ref[...] = kv


def attend_grads(pair, joined, branch, dkv, dquery, qm, patch):
    total, rows, width = joined.shape
    lat, cols = rows - patch, dkv.shape[2]
    steps = row_tiles(width)
    tile = pl.BlockSpec((width // steps, cols), lambda i: (i, 0))
    return pl.pallas_call(
        functools.partial(attend_grads_kernel, patch, HEAD ** (-0.5)),
        grid=(steps,),
        in_specs=[
            SMALL,
            pl.BlockSpec((total, rows, width // steps), lambda i: (0, 0, i)),
            pl.BlockSpec((total * lat, width // steps), lambda i: (0, i)),
            whole(dkv.shape), whole(dquery.shape), whole(qm.shape),
        ],
        out_specs=[tile] + [whole((width // steps, cols))] * steps,
        out_shape=[jax.ShapeDtypeStruct((width, cols), BF16)] + [jax.ShapeDtypeStruct((width // steps, cols), BF16)] * steps,
        compiler_params=pltpu.CompilerParams(vmem_limit_bytes=VMEM),
        cost_estimate=LITTLE,
    )(pair, joined, branch, dkv, dquery, qm)


def whole(shape):
    return pl.BlockSpec(shape, lambda *_: (0,) * len(shape))


def once(kernel, operands, shapes, cost=LITTLE, limit=VMEM):
    return pl.pallas_call(
        kernel,
        grid=(1,),
        in_specs=[whole(operand.shape) for operand in operands],
        out_specs=[whole(shape) for shape, _ in shapes],
        out_shape=[jax.ShapeDtypeStruct(shape, kind) for shape, kind in shapes],
        compiler_params=pltpu.CompilerParams(vmem_limit_bytes=limit),
        cost_estimate=cost,
    )(*operands)


def attended_kernel(small_ref, latent_ref, *refs):
    *part_refs, attended_ref, hidden_ref = refs
    images = latent_ref.shape[0]
    each = len(part_refs) // images
    for image in range(images):
        total = latent_ref[image].astype(F32)
        for part_ref in part_refs[image * each : (image + 1) * each]:
            total = total + part_ref[0].astype(F32)
        attended_ref[image] = total
        hidden_ref[image] = normed(total, small_ref[0, 2:3], small_ref[1, 2:3]).astype(BF16)


def summed_kernel(first_ref, second_ref, *to_refs):
    rows = to_refs[0].shape[0]
    for index, to_ref in enumerate(to_refs):
        place = slice(index * rows, (index + 1) * rows)
        to_ref[...] = (first_ref[place].astype(F32) + second_ref[place].astype(F32)).astype(BF16)


def through_kernel(*refs):
    for index in range(2):
        left_ref, right_ref, to_ref = refs[2 * index], refs[2 * index + 1], refs[4 + index]
        to_ref[...] = (left_ref[...].astype(F32) + right_ref[...].astype(F32)).astype(BF16)


def norm_back(rows, gain, grad):
    average = jnp.mean(rows, axis=-1, keepdims=True)
    centred = rows - average
    inverse = lax.rsqrt(jnp.mean(centred * centred, axis=-1, keepdims=True) + EPSILON)
    unit = centred * inverse
    scaled = grad * gain
    first = jnp.mean(scaled, axis=-1, keepdims=True)
    second = jnp.mean(scaled * unit, axis=-1, keepdims=True)
    back = inverse * (scaled - first - unit * second)
    return back, jnp.sum(grad * unit, axis=0, keepdims=True), jnp.sum(grad, axis=0, keepdims=True)


def branch_kernel(small_ref, attended_ref, cot_ref, *refs):
    *part_refs, grad_ref, branch_ref, sums_ref = refs
    images, lat, width = attended_ref.shape
    grad = sum(part_ref[...].astype(F32) for part_ref in part_refs)
    back, gain, bias = norm_back(attended_ref[...].reshape(images * lat, width), small_ref[0, 2:3], grad)
    total = (cot_ref[...].reshape(images * lat, width).astype(F32) + back).reshape(images, lat, width)
    grad_ref[...] = total
    branch_ref[...] = total.astype(BF16)
    sums_ref[0:1] = gain
    sums_ref[1:2] = bias


def rows_back_kernel(small_ref, sums_two_ref, media_ref, latent_ref, grad_ref, *refs):
    *part_refs, media_to_ref, latent_to_ref, sums_ref = refs
    images, patch, _ = media_ref.shape
    each = len(part_refs) // images
    totals = None
    for image in range(images):
        parts = part_refs[image * each : (image + 1) * each]
        grad = sum(part_ref[0, :patch].astype(F32) for part_ref in parts)
        media, gain_zero, bias_zero = norm_back(media_ref[image].astype(F32), small_ref[0, 0:1], grad)
        media_to_ref[image] = media
        grad = sum(part_ref[0, patch:].astype(F32) for part_ref in parts)
        latent, gain_one, bias_one = norm_back(latent_ref[image].astype(F32), small_ref[0, 1:2], grad)
        latent_to_ref[image] = grad_ref[image] + latent
        terms = gain_zero, gain_one, bias_zero, bias_one
        totals = terms if totals is None else [left + right for left, right in zip(totals, terms)]
    for row, total in zip((0, 1, 3, 4), totals):
        sums_ref[row : row + 1] = total
    sums_ref[2:3] = sums_two_ref[0:1]
    sums_ref[5:6] = sums_two_ref[1:2]


def in_thirds(values):
    parts, rest = [], values
    for _ in range(3):
        part = lax.reduce_precision(rest, exponent_bits=8, mantissa_bits=7)
        parts.append(part.astype(BF16))
        rest = rest - part
    return jnp.stack(parts)


def local(media_features, latents, cotangent, image_counts, w_query, w_key, w_value, w_out, w_up, w_down,
          norm_gains, norm_biases):
    devices_x, devices_y = lax.axis_size("gx"), lax.axis_size("gy")
    masks = far_masks()
    img_count, lat, width = latents.shape
    patch = media_features.shape[1]
    rows = patch + lat
    shard = w_query.shape[0]
    head_width = width // devices_y
    heads = 2 * head_width // HEAD
    pair = (lax.axis_index("gy") % 2).astype(jnp.int32).reshape(1)
    ff_width = w_up.shape[1] // devices_y
    total = img_count * len(masks)

    four_width = 4 * head_width
    small = in_thirds(jnp.stack([norm_gains, norm_biases])).reshape(-1)
    extra = -(-small.size // (16 * four_width)) * 16
    small = jnp.pad(small, (0, extra * four_width - small.size)).reshape(extra, four_width)
    four = regroup(small, devices_y, w_key, w_value, w_query, w_out.T)
    four = lax.all_to_all(four, "gy", split_axis=0, concat_axis=0, tiled=True)
    mine = lax.all_gather(four[:, extra:].reshape(devices_y * shard, four_width), "gx", axis=0, tiled=True)

    two = jnp.concatenate(
        [part.reshape(shard, devices_y, ff_width).transpose(1, 0, 2) for part in (w_up, w_down.T)], axis=2
    )
    two, four = tie(two, four)
    small = four[:, :extra].reshape(devices_y, -1)[:, : 18 * shard].reshape(devices_y, 3, 6 * shard)
    small = gather_small(jnp.sum(small.astype(F32), axis=1).reshape(1, -1), "gx")
    small = small.reshape(devices_x, devices_y, 6, shard).transpose(2, 0, 1, 3).reshape(2, 3, width)

    two = lax.all_to_all(two, "gy", split_axis=0, concat_axis=0, tiled=True)
    live = (jnp.arange(img_count, dtype=jnp.int32) < image_counts[0]).astype(BF16)
    cot_own = cotangent * live[:, None, None]
    own = [
        jnp.concatenate([part[i : i + 1] for part in (media_features, latents, cot_own)], axis=1) for i in range(img_count)
    ]
    two, small, *own = tie(two, small, *own)
    ff_rows = two.reshape(devices_y * shard, 2 * ff_width)
    gains, biases = small[0], small[1]

    raw = {(0, i): own[i] for i in range(img_count)}
    if len(masks) == 4 and img_count == 2:
        slots = [(0, 0), (0, 1), (2, 0), (4, 0), (2, 1), (4, 1), (6, 0), (6, 1)]
        raw[2, 0], raw[4, 0], later = tie(swap(own[0], 2), swap(own[0], 4), own[1])
        raw[2, 0], raw[4, 0], ff_rows, mine = tie(raw[2, 0], raw[4, 0], ff_rows, mine)
        raw[2, 1], raw[4, 1], raw[6, 0] = swap(later, 2), swap(later, 4), swap(raw[2, 0], 4)
    else:
        slots = [(mask, i) for mask in masks for i in range(img_count)]
        for mask in masks[1:]:
            raw.update({(mask, i): swap(own[i], mask) for i in range(img_count)})
    ff_mine = lax.all_gather(ff_rows, "gx", axis=0, tiled=True)
    theirs = swap(mine, 1)

    steps, carried, out_parts = total // img_count, None, {}
    for step in range(steps):
        here = slots[step * img_count : (step + 1) * img_count]
        if carried:
            carried[0], *raws = tie(carried[0], *[raw[slot] for slot in here])
            raw.update(dict(zip(here, raws)))
        if (4, 1) in here and (6, 1) not in raw:
            raw[6, 1] = swap(raw[4, 1], 2)
        *carried, first_part, second_part = attend(
            pair, mine, theirs, small, [raw[slot] for slot in here], heads, patch, rows, step, total, carried
        )
        out_parts.update(dict(zip(here, (first_part, second_part))))
    joined_all, kv_all, qm_all = carried

    qm_all, *parts = tie(qm_all, *[raw[mask, i] for mask in masks for i in range(img_count)])
    cot_own_all = pick(parts, rows // lat, lat)
    out_parts = [
        swap(out_parts[mask, i], mask) if mask else out_parts[mask, i] for i in range(img_count) for mask in masks
    ]
    like_latents = lambda kind: (latents.shape, kind)
    attended, hidden_own = once(
        attended_kernel, [small, latents, *out_parts], [like_latents(F32), like_latents(BF16)]
    )
    hidden_own, cot_own_all = tie(hidden_own, cot_own_all)
    cot_other = swap(cot_own_all, 1)
    hidden = [part.reshape(img_count * lat, width) for part in spread(hidden_own).values()]
    hidden.append(swap(jnp.concatenate(hidden), 1))

    def plus(left, right):
        return (left.astype(F32) + right.astype(F32)).astype(BF16)

    def collect_pairs(parts):
        parts = [part.reshape(img_count, lat, width) for part in parts]
        return [parts[0]] + [swap(part, mask) for mask, part in zip(masks[1:], parts[1:])]

    total_of = lambda parts: sum(part.astype(F32) for part in parts)

    def summed(own, other):
        return once(summed_kernel, [own, swap(other, 1)], [((img_count * lat, width), BF16)] * len(masks))

    hidden, cot_all, active, grad_upper, hidden_parts, hidden_other = feed(hidden, cot_own_all, cot_other, ff_mine)
    hidden_parts = summed(hidden_parts, hidden_other)
    grad_upper, *hidden_parts = tie(grad_upper, *hidden_parts)
    ff_grads = feed_grads(hidden, cot_all, grad_upper, active)
    ff_part = lax.psum_scatter(ff_grads, "gx", scatter_dimension=0, tiled=True)
    hidden_parts = collect_pairs(hidden_parts)
    hidden_parts = [part.reshape(img_count * lat, width) for part in hidden_parts]
    grad_attended, grad_branch, sums_two = once(
        branch_kernel, [small, attended, cot_own, *hidden_parts],
        [like_latents(F32), like_latents(BF16), ((2, width), F32)], limit=MOST,
    )
    branch = spread(grad_branch)
    ffn_parts = feed_out(active, ff_mine)
    *branch, ffn_part, ffn_other = tie(*branch.values(), *ffn_parts)
    branch = jnp.concatenate([branch[masks.index(mask)][i : i + 1] for mask, i in slots])

    arrays = pair, mine, theirs, branch, kv_all, qm_all, heads, patch
    back, carried, step = {}, None, steps - 1
    for count in (1, steps - 1):
        *carried, results = attend_back(*arrays, step, count, img_count, carried)
        for index, part in enumerate(results):
            back[slots[(step - index // img_count) * img_count + index % img_count]] = part
        step -= count
    dkv_all, dquery_all = carried

    if len(masks) == 4 and img_count == 2:
        last = swap(back[6, 0], 4), swap(back[6, 1], 2)
        through = once(
            through_kernel, [back[2, 0], last[0], back[4, 1], last[1]], [(back[2, 0].shape, BF16)] * 2
        )
        dkv_all, *through = tie(dkv_all, *through)
    def home(part):
        return lax.all_to_all(part.reshape(devices_y, shard, -1), "gy", split_axis=0, concat_axis=0, tiled=True)

    keep, *give = attend_grads(
        pair, joined_all, branch.reshape(total * lat, width), dkv_all, dquery_all, qm_all, patch
    )
    if len(masks) == 4 and img_count == 2:
        keep, ff_part, *through = tie(keep, ff_part, swap(through[0], 2), swap(through[1], 4), back[4, 0], back[2, 1])
        direct = swap(through[2], 4), swap(through[3], 2)
        arrived = [back[0, 0], through[0], direct[0], back[0, 1], direct[1], through[1]]
    else:
        arrived = [swap(back[mask, i], mask) if mask else back[mask, i] for i in range(img_count) for mask in masks]
    give = [swap(part, 1) for part in give]
    (at_grads,) = once(add_pieces_kernel, [keep, *give], [(keep.shape, BF16)])
    at_grads, ffn_other = tie(at_grads, ffn_other)
    shares = lax.psum_scatter(at_grads, "gx", scatter_dimension=0, tiled=True)
    ffn_parts = summed(ffn_part, ffn_other)

    each = len(arrived)
    *arrived, ff_part = tie(*arrived, *ffn_parts, ff_part)
    arrived, ffn_parts = arrived[:each], arrived[each:]
    grad_media, grad_latents, sums = once(
        rows_back_kernel, [small, sums_two, media_features, latents, grad_attended, *arrived],
        [(media_features.shape, F32), like_latents(F32), ((6, width), F32)],
        cost=SOME, limit=MOST,
    )
    sums = sums + swap(sums, 1)
    sums = sum([sums] + [swap(sums, mask) for mask in masks[1:]])
    sums, *ffn_parts = tie(sums, *ffn_parts)
    ffn_parts = collect_pairs(ffn_parts)
    sums = sum([sums] + [swap(sums, mask, "gx") for mask in range(1, devices_x)])
    place = lax.axis_index("gx") * devices_y + lax.axis_index("gy")
    sums = lax.dynamic_slice_in_dim(sums, place * shard, shard, axis=1)

    shares, sums, ff_part, *ffn_parts = tie(shares, sums, home(ff_part), *ffn_parts)
    grad_key, grad_value, grad_query, grad_out = ungroup(home(shares), 4, True)
    outputs = ((attended + total_of(ffn_parts)) * live.astype(F32)[:, None, None]).astype(BF16)
    grad_up, grad_down = ungroup(ff_part, 2, False, SOME)
    grad_down = grad_down.T
    return (
        outputs, grad_media, grad_latents, grad_query, grad_key, grad_value, grad_out.T, grad_up, grad_down,
        sums[:3], sums[3:],
    )


def solution(mesh):
    split = ("gx", "gy")
    images, first, second = P(split, None, None), P(split, None), P(None, split)
    return jax.shard_map(
        local,
        mesh=mesh,
        in_specs=(images, images, images, P(split), first, first, first, second, first, second, second, second),
        out_specs=(images, images, images, first, first, first, second, first, second, second, second),
        check_vma=False,
    )
```
